256 devices in a mesh: amp: 32 (over y, x, core), int: 8 (over z).
Axes of the slice: x: 4, y: 4, z: 8, core: 2. Of those that a mesh axis runs over, the one named last changes fastest.
Arguments:
- amplitudes: float32 [1536, 1024], P('int'), may hold values from -6 to 6
- slab_integrals: float32 [1024, 51200], P('int', 'amp'), may hold values from -0.1875 to 0.1875
- cycle_integrals: float32 [96, 800, 1024], P('int', 'amp'), may hold values from -0.0390625 to 0.0390625
- occ_irrep: int32 [96], replicated, may hold values from 0 to 7
- vir_irrep: int32 [800], replicated, may hold values from 0 to 7
Outputs:
- ladder: float32 [1536, 51200], P('int', 'amp')
- cycle: float32 [1024, 1024], P('int', 'amp')
The draws below stay inside these ranges and needn't reach their ends.
All inputs are finite; a program needn't handle non-finite values.
Results may differ from the reference program's by a relative error of at most 0.00011.
Values sent between devices are 32-bit elements; how exact they have to be, the bound alone decides.
A program may use at most 64 MiB of HBM per device.

```python
import jax
import jax.numpy as jnp
from jax import lax

NOCC = 96
NVIR = 800
SLAB = 64
IBAT = 16
PW = 1024
ROWS = 1536


def with_ends(entries, own_key, low, largest):
    dims = entries.shape
    place = [jax.random.randint(jax.random.fold_in(own_key, axis), (), 0, dims[axis]) for axis in range(len(dims))]
    entries = entries.at[tuple(place)].set(low)
    longest = dims.index(max(dims))
    place[longest] = (place[longest] + 1) % dims[longest]
    return entries.at[tuple(place)].set(largest)


def strengthened(array, own_key, source, target, blocks, factor):
    def block_of(axis_at):
        return (jnp.arange(array.shape[axis_at]) // (array.shape[axis_at] // blocks)).reshape((-1,) + (1,) * (array.ndim - 1 - axis_at))

    one_side = jax.random.permutation(own_key, blocks)[block_of(target)]
    other_side = (block_of(target) + blocks // 2) % blocks
    return jnp.where((block_of(source) == one_side) | (block_of(source) == other_side), factor * array, array)


def shard_levels(key, extent, shards, least, largest):
    gain = 1.0
    for position, shards_of in shards:
        heights = jax.random.uniform(jax.random.fold_in(jax.random.fold_in(key, 6), position), (shards_of,), jnp.float32, least / len(shards), largest / len(shards))
        gain = gain * jnp.repeat(jnp.exp(heights), extent[position] // shards_of).reshape((-1,) + (1,) * (len(extent) - 1 - position))
    return gain


def noise(stream_key, shape, width, most, split=(), kind=jnp.bfloat16):
    loudness = shard_levels(stream_key, shape, split, -0.22, 0.18) if split else 1.0
    drawn = jax.random.normal(stream_key, shape, jnp.float32) * width * loudness
    return jnp.minimum(jnp.maximum(drawn, -most), most).astype(kind)


def gaussian_with(rng, extent, width, bound, pieces, heavy, dtype=jnp.bfloat16):
    values = width * jax.random.normal(rng, extent, jnp.float32)
    if pieces:
        values = values * shard_levels(rng, extent, pieces, -0.22, 0.18)
    return jnp.clip(strengthened(values, jax.random.fold_in(rng, 3), *heavy), -bound, bound).astype(dtype)


def setup_inputs(seed: int = 0) -> dict:
    keys = jax.random.split(jax.random.key(seed), 6)
    return {
        "amplitudes": noise(keys[0], (ROWS, PW), 1.0, 6.0, ((0, 8),), jnp.float32),
        "slab_integrals": noise(keys[1], (PW, SLAB * NVIR), PW ** -0.5, 0.1875, ((0, 8), (1, 32)), jnp.float32),
        "cycle_integrals": gaussian_with(keys[2], (NOCC, NVIR, IBAT * SLAB), (NOCC * NVIR) ** -0.5, 0.0390625, ((0, 8), (1, 32)), (1, 2, 32, 2.75), jnp.float32),
        "occ_irrep": with_ends(jax.random.randint(keys[3], (NOCC,), 0, 8), jax.random.fold_in(keys[3], 1), 0, 7).astype(jnp.int32),
        "vir_irrep": with_ends(jax.random.randint(keys[4], (NVIR,), 0, 8), jax.random.fold_in(keys[4], 1), 0, 7).astype(jnp.int32),
    }


def reference(amplitudes, slab_integrals, cycle_integrals, occ_irrep, vir_irrep):
    ladder = jnp.dot(amplitudes, slab_integrals, precision=lax.Precision.HIGHEST, preferred_element_type=jnp.float32)
    blocks = ladder.reshape(IBAT, NOCC, SLAB, NVIR)
    sums = jnp.einsum("ikac,kcn->ian", blocks, cycle_integrals, precision=lax.Precision.HIGHEST)
    sums = sums.reshape(IBAT * SLAB, IBAT * SLAB)
    labels = jnp.bitwise_xor(occ_irrep[:IBAT][:, None], vir_irrep[:SLAB][None, :]).reshape(-1)
    keep = labels[:, None] == labels[None, :]
    cycle = jnp.where(keep, sums, jnp.zeros_like(sums))
    return ladder, cycle
```

```python
import jax
import jax.numpy as jnp
from jax import lax
from jax.experimental import pallas as pl
from jax.experimental.pallas import tpu as pltpu
from jax.sharding import PartitionSpec as P

NOCC = 96
NVIR = 800
SLAB = 64
F32 = jnp.float32
BF16 = jnp.bfloat16
MESH = pl.DeviceIdType.MESH

AMP = 32
INT = 8
W0 = 896
W1 = 704
CUT1 = 768
WIDTHS = (W0, W1)
STARTS = (0, W0)
RIGHT, LEFT = 0, 1


def iota(shape, dim):
    return lax.broadcasted_iota(jnp.int32, shape, dim)


def split(x):
    high = x.astype(BF16)
    return high, (x - high.astype(F32)).astype(BF16)


def mm(a, b):
    return jnp.dot(a, b, preferred_element_type=F32)


def mm_nt(a, b):
    return lax.dot_general(a, b, (((1,), (1,)), ((), ())), preferred_element_type=F32)


def one_hot(match):
    return jnp.where(match, 1.0, 0.0).astype(BF16)


def body(
    amp_ref, slab_ref, w_ref,
    lad_ref, sum_ref,
    g0, g1, a3, l2, l2h, l2l, p0, p1, s_buf, t_buf, u_buf, v_buf,
    wpad, wx, whi, wlo, msg, rcv, ct, rs, sxy, zs, zr,
    ag_send, ag_recv, s_sem, u_sem, w_sem, a_send, a_recv, r_send, r_recv, z_sem,
):
    d = lax.axis_index("amp")
    z = lax.axis_index("int")
    core = lax.rem(d, 2)
    chip = d // 2
    row = d // 8
    tile = lax.rem(d, 8)
    sibling = d + 1 - 2 * core
    gather = (g0, g1)
    spread = (p0, p1)

    def around(step):
        return lax.rem(z + step + INT, INT)

    barrier = pltpu.get_barrier_semaphore()

    @pl.loop(1, AMP)
    def _(j):
        pl.semaphore_signal(barrier, inc=1, device_id={"amp": lax.rem(d + j, AMP), "int": z}, device_id_type=MESH)

    @pl.loop(1, INT)
    def _(j):
        up = lax.rem(z + j, INT)
        pl.semaphore_signal(barrier, inc=1, device_id={"amp": d, "int": up}, device_id_type=MESH)
        pl.semaphore_signal(barrier, inc=1, device_id={"amp": sibling, "int": up}, device_id_type=MESH)

    pl.semaphore_wait(barrier, AMP - 1 + 2 * (INT - 1))

    def piece(way, s, j, h):
        hop = 1 if way == RIGHT else -1
        origin = around(-hop * (j - 1))
        rows = pl.ds(64 * h, 64)
        target = gather[s].at[origin, rows, :]
        if j == 1:
            source = slab_ref.at[rows, pl.ds(STARTS[s], WIDTHS[s])]
        else:
            source = target
        k = ((way * 2 + s) * 4 + (j - 1)) * 2 + h
        return pltpu.make_async_remote_copy(
            src_ref=source, dst_ref=target, send_sem=ag_send.at[k], recv_sem=ag_recv.at[k],
            device_id={"amp": d, "int": around(hop)}, device_id_type=MESH,
        )

    started = []

    def launch(way, s, j, h):
        copy = piece(way, s, j, h)
        copy.start()
        started.append(copy)

    def arrived(way, s, j, h):
        hop = 1 if way == RIGHT else -1
        origin = around(-hop * j)
        target = gather[s].at[origin, pl.ds(64 * h, 64), :]
        k = ((way * 2 + s) * 4 + (j - 1)) * 2 + h
        pltpu.make_async_copy(target, target, ag_recv.at[k]).wait()

    def begin(s):
        for h in range(2):
            for way in (RIGHT, LEFT):
                launch(way, s, 1, h)

    def event(s, j, h):
        for way in (RIGHT, LEFT):
            arrived(way, s, j, h)
            if j < 3 or h == way:
                launch(way, s, j + 1, h)

    def last(s):
        arrived(RIGHT, s, 4, 0)
        arrived(LEFT, s, 4, 1)

    def process(s, origin, own):
        a_block = a3[origin]
        start, width = STARTS[s], WIDTHS[s]

        def step(col, n):
            if own:
                b = slab_ref[:, pl.ds(start + col, n)]
            else:
                b = gather[s][origin, :, pl.ds(col, n)]
            high, low = split(b)
            part = mm(a_block, jnp.concatenate([high, high, low], axis=0))
            into = pl.ds(start + col, n)
            if own:
                lad_ref[:, into] = part[:192]
                l2[:, into] = part[192:]
            else:
                lad_ref[:, into] += part[:192]
                l2[:, into] += part[192:]

        full = width // 256

        @pl.loop(0, full)
        def _(i):
            step(pl.multiple_of(i * 256, 256), 256)

        step(full * 256, width - full * 256)

    begin(0)

    here = pl.ds(pl.multiple_of(tile * 128, 128), 128)
    r, c = iota((256, 192), 0), iota((256, 192), 1)
    pick = one_hot((c == 96 * ((r >> 4) & 1) + 12 * (r >> 5) + (r & 15)) & ((r & 15) < 12))
    high, low = split(amp_ref[:, here])
    s_buf[...] = (mm(pick, high) + mm(pick, low)).reshape(INT, 32, 128)

    def s_copy(up):
        return pltpu.make_async_remote_copy(
            src_ref=s_buf.at[up], dst_ref=t_buf.at[z], send_sem=s_sem.at[0], recv_sem=s_sem.at[1],
            device_id={"amp": d, "int": up}, device_id_type=MESH,
        )

    @pl.loop(1, INT)
    def _(j):
        s_copy(lax.rem(z + j, INT)).start()

    t_buf[z] = s_buf[z]

    wpad[...] = jnp.zeros_like(wpad)
    for k in range(12):
        wpad[pl.ds(32 * k, 25), :] = w_ref[k]

    @pl.loop(0, 8)
    def _(i):
        at = pl.ds(pl.multiple_of(i * 128, 128), 128)
        for k4 in range(3):
            wx[core, at, 128 * k4 : 128 * k4 + 128] = wpad[128 * k4 : 128 * k4 + 128, at].T

    w_copy = pltpu.make_async_remote_copy(
        src_ref=wx.at[core], dst_ref=wx.at[core], send_sem=w_sem.at[0], recv_sem=w_sem.at[1],
        device_id={"amp": sibling, "int": z}, device_id_type=MESH,
    )
    w_copy.start()

    seven = pl.ds(0, INT - 1)
    pltpu.make_async_copy(s_buf.at[seven], t_buf.at[seven], s_sem.at[1]).wait()
    r, c = iota((192, 256), 0), iota((192, 256), 1)
    pick = one_hot(c == 32 * ((r >> 1) & 7) + 16 * (r & 1) + (r >> 4))
    high, low = split(t_buf[...].reshape(256, 128))
    u_buf[...] = mm(pick, high) + mm(pick, low)

    @pl.loop(1, 8)
    def _(j):
        pltpu.make_async_remote_copy(
            src_ref=u_buf, dst_ref=v_buf.at[tile], send_sem=u_sem.at[0], recv_sem=u_sem.at[1],
            device_id={"amp": row * 8 + lax.rem(tile + j, 8), "int": z}, device_id_type=MESH,
        ).start()

    v_buf[tile] = u_buf[...]
    event(0, 1, 0)

    for o in range(INT):
        high, low = split(amp_ref[:, 128 * o : 128 * o + 128])
        a3[o, :192, 0:128] = high
        a3[o, :192, 128:256] = low
        a3[o, :192, 256:384] = high

    for n, ref in enumerate(spread):
        @pl.loop(0, ref.shape[0] // 64)
        def _(i):
            c = iota((64, 1024), 0) + (i * 64 - 32 * n)
            l = iota((64, 1024), 1)
            ref[pl.ds(pl.multiple_of(i * 64, 64), 64), :] = one_hot((c == 25 * (l >> 5) + (l & 31)) & ((l & 31) < 25))

    event(0, 1, 1)

    pltpu.make_async_copy(v_buf.at[seven], v_buf.at[seven], u_sem.at[1]).wait()

    @pl.loop(0, INT)
    def _(o):
        high, low = split(v_buf[o])
        a3[o, 192:, 0:128] = high
        a3[o, 192:, 128:256] = low
        a3[o, 192:, 256:384] = high

    event(0, 2, 0)
    process(0, z, True)
    process(0, around(-1), False)
    event(0, 2, 1)
    process(0, around(1), False)
    process(0, around(-2), False)
    event(0, 3, 0)
    process(0, around(2), False)

    w_copy.wait_recv()

    @pl.loop(0, 8)
    def _(i):
        at = pl.ds(pl.multiple_of(i * 128, 128), 128)
        for n in range(2):
            high, low = split(wx[n, at, :])
            whi[at, 384 * n : 384 * n + 384] = high
            wlo[at, 384 * n : 384 * n + 384] = low

    event(0, 3, 1)
    begin(1)
    process(0, around(-3), False)
    process(0, around(3), False)
    last(0)
    process(0, around(4), False)

    def regroup(a):
        win = pl.ds(0, W0) if a == 0 else pl.ds(CUT1, 832)
        size = 896 if a == 0 else 832
        high, low = split(l2[:, win])
        l2h[:, :size] = high
        l2l[:, :size] = low
        lane = iota((16, 128), 1)
        even = (lane & 32) == 0
        lower = (lane & 64) == 0

        @pl.loop(0, 4)
        def _(tp):
            cols = pl.ds(pl.multiple_of(tp * 256, 256), 256)
            table = spread[a][:, cols]
            spaced = mm(l2h[:, :size], table) + mm(l2l[:, :size], table)
            for gg in range(2):
                g = tp * 2 + gg
                for k4 in range(3):
                    x = [spaced[(4 * k4 + q) * 16 : (4 * k4 + q) * 16 + 16, 128 * gg : 128 * gg + 128] for q in range(4)]
                    y = [None] * 4
                    for q in (0, 2):
                        y[q] = jnp.where(even, x[q], pltpu.roll(x[q + 1], 32, 1))
                        y[q + 1] = jnp.where(even, pltpu.roll(x[q], 96, 1), x[q + 1])
                    o = [None] * 4
                    for q in (0, 1):
                        o[q] = jnp.where(lower, y[q], pltpu.roll(y[q + 2], 64, 1))
                        o[q + 2] = jnp.where(lower, pltpu.roll(y[q], 64, 1), y[q + 2])
                    for s in range(4):
                        lanes = pl.ds(384 * (s % 2) + 128 * k4, 128)
                        for hh in range(2):
                            msg[a, 4 * g + 2 * (s // 2) + hh, :, lanes] = o[s][8 * hh : 8 * hh + 8]

        @pl.loop(1, AMP)
        def _(j):
            to = lax.rem(d + j, AMP)
            pltpu.make_async_remote_copy(
                src_ref=msg.at[a, to], dst_ref=rcv.at[a, d], send_sem=a_send.at[a], recv_sem=a_recv.at[a],
                device_id={"amp": to, "int": z}, device_id_type=MESH,
            ).start()

        rcv[a, d] = msg[a, d]

    others = pl.ds(0, AMP - 1)

    def contract(a):
        pltpu.make_async_copy(msg.at[a, others], rcv.at[a, others], a_recv.at[a]).wait()
        r, c = iota((256, 256), 0), iota((256, 256), 1)
        pick = one_hot(c == ((r & 63) >> 1) * 8 + 2 * (r >> 6) + (r & 1))
        high, low = split(rcv[a].reshape(256, 768))
        high = mm(pick, high).astype(BF16)
        low = mm(pick, low).astype(BF16)

        @pl.loop(0, 4)
        def _(q):
            quarter = lax.rem(row + q, 4)
            at = pl.ds(pl.multiple_of(quarter * 256, 256), 256)
            wh, wl = whi[at, :], wlo[at, :]
            part = mm_nt(wh, high) + (mm_nt(wl, high) + mm_nt(wh, low))
            ct[a, pl.ds(quarter * 4, 4)] = part.reshape(4, 64, 256)
            for n in range(4):
                to = quarter * 4 + lax.rem(chip + n, 4)

                @pl.when(to != chip)
                def _():
                    pltpu.make_async_remote_copy(
                        src_ref=ct.at[a, to], dst_ref=rs.at[a, chip], send_sem=r_send.at[a], recv_sem=r_recv.at[a],
                        device_id={"amp": to * 2 + core, "int": z}, device_id_type=MESH,
                    ).start()

        rs[a, chip] = ct[a, chip]

    fifteen = pl.ds(0, 15)

    def narrow(a):
        pltpu.make_async_copy(ct.at[a, fifteen], rs.at[a, fifteen], r_recv.at[a]).wait()
        sxy[...] = rs[a, 0]

        @pl.loop(1, 16)
        def _(n):
            sxy[...] += rs[a, n]

        for cc in range(2):
            for zz in range(4):
                zs[cc * 4 + zz, :, 64 * a : 64 * a + 64] = sxy[32 * cc : 32 * cc + 32, 64 * zz : 64 * zz + 64]

    regroup(0)
    event(1, 1, 0)
    process(1, z, True)
    event(1, 1, 1)
    process(1, around(-1), False)
    process(1, around(1), False)
    event(1, 2, 0)
    event(1, 2, 1)
    contract(0)
    process(1, around(-2), False)
    event(1, 3, 0)
    process(1, around(2), False)
    event(1, 3, 1)
    process(1, around(-3), False)
    process(1, around(3), False)
    last(1)
    process(1, around(4), False)
    regroup(1)
    narrow(0)
    contract(1)
    narrow(1)

    @pl.loop(0, 8)
    def _(n):
        to = chip * 2 + n // 4
        up = core * 4 + lax.rem(n, 4)
        mine = (to == d) & (up == z)

        @pl.when(jnp.logical_not(mine))
        def _():
            pltpu.make_async_remote_copy(
                src_ref=zs.at[n], dst_ref=zr.at[z], send_sem=z_sem.at[0], recv_sem=z_sem.at[1],
                device_id={"amp": to, "int": up}, device_id_type=MESH,
            ).start()

        @pl.when(mine)
        def _():
            zr[z] = zs[n]

    local = core == z // 4

    @pl.when(local)
    def _():
        pltpu.make_async_copy(zs.at[seven], zr.at[seven], z_sem.at[1]).wait()
        pltpu.make_async_copy(zs.at[seven], zr.at[seven], z_sem.at[0]).wait()

    @pl.when(jnp.logical_not(local))
    def _():
        pltpu.make_async_copy(zs, zr, z_sem.at[1]).wait()
        pltpu.make_async_copy(zs, zr, z_sem.at[0]).wait()

    total = zr[0]
    for n in range(1, INT):
        total += zr[n]
    r, c = iota((128, 128), 0), iota((128, 128), 1)
    order = jnp.where(c == 64 * (r & 1) + 2 * ((r & 63) >> 1) + (r >> 6), 1.0, 0.0).astype(F32)
    sum_ref[...] = lax.dot_general(
        order, total, (((1,), (1,)), ((), ())), precision=lax.Precision.HIGHEST, preferred_element_type=F32
    )

    for copy in started:
        copy.wait_send()
    pltpu.make_async_copy(s_buf.at[seven], t_buf.at[seven], s_sem.at[0]).wait()
    pltpu.make_async_copy(v_buf.at[seven], v_buf.at[seven], u_sem.at[0]).wait()
    w_copy.wait_send()
    for a in range(2):
        pltpu.make_async_copy(msg.at[a, others], rcv.at[a, others], a_send.at[a]).wait()
        pltpu.make_async_copy(ct.at[a, fifteen], rs.at[a, fifteen], r_send.at[a]).wait()


def fused(amplitudes, slab_integrals, cycle_integrals):
    vmem = pl.BlockSpec(memory_space=pltpu.VMEM)
    dma = pltpu.SemaphoreType.DMA
    return pl.pallas_call(
        body,
        out_shape=(
            jax.ShapeDtypeStruct((192, 1600), F32),
            jax.ShapeDtypeStruct((128, 32), F32),
        ),
        in_specs=[vmem] * 3,
        out_specs=(vmem, vmem),
        scratch_shapes=[
            pltpu.VMEM((INT, 128, W0), F32),
            pltpu.VMEM((INT, 128, W1), F32),
            pltpu.VMEM((INT, 384, 384), BF16),
            pltpu.VMEM((192, 1600), F32),
            pltpu.VMEM((192, 896), BF16),
            pltpu.VMEM((192, 896), BF16),
            pltpu.VMEM((896, 1024), BF16),
            pltpu.VMEM((832, 1024), BF16),
            pltpu.VMEM((INT, 32, 128), F32),
            pltpu.VMEM((INT, 32, 128), F32),
            pltpu.VMEM((192, 128), F32),
            pltpu.VMEM((INT, 192, 128), F32),
            pltpu.VMEM((384, 1024), F32),
            pltpu.VMEM((2, 1024, 384), F32),
            pltpu.VMEM((1024, 768), BF16),
            pltpu.VMEM((1024, 768), BF16),
            pltpu.VMEM((2, AMP, 8, 768), F32),
            pltpu.VMEM((2, AMP, 8, 768), F32),
            pltpu.VMEM((2, 16, 64, 256), F32),
            pltpu.VMEM((2, 16, 64, 256), F32),
            pltpu.VMEM((64, 256), F32),
            pltpu.VMEM((8, 32, 128), F32),
            pltpu.VMEM((INT, 32, 128), F32),
            dma((32,)),
            dma((32,)),
            dma((2,)),
            dma((2,)),
            dma((2,)),
            dma((2,)),
            dma((2,)),
            dma((2,)),
            dma((2,)),
            dma((2,)),
        ],
        compiler_params=pltpu.CompilerParams(
            collective_id=0, has_side_effects=True, vmem_limit_bytes=58 * 1024 * 1024
        ),
        cost_estimate=pl.CostEstimate(flops=8_000_000_000, bytes_accessed=8_000_000, transcendentals=0),
    )(amplitudes, slab_integrals, cycle_integrals)


def per_device(amplitudes, slab_integrals, cycle_integrals, occ_irrep, vir_irrep):
    ladder, sums = fused(amplitudes, slab_integrals, cycle_integrals)
    i_local = 2
    col_local = sums.shape[1]
    row_start = lax.axis_index("int") * i_local
    batch_labels = lax.dynamic_slice_in_dim(occ_irrep, row_start, i_local, 0)
    slab_labels = vir_irrep[:SLAB]
    row_labels = jnp.bitwise_xor(batch_labels[:, None], slab_labels[None, :]).reshape(-1)
    col_ids = lax.axis_index("amp") * col_local + jnp.arange(col_local, dtype=jnp.int32)
    col_occ = col_ids // SLAB
    col_vir = col_ids % SLAB
    occ_match = col_occ[:, None] == jnp.arange(NOCC, dtype=jnp.int32)[None, :]
    vir_match = col_vir[:, None] == jnp.arange(SLAB, dtype=jnp.int32)[None, :]
    occ_lookup = jnp.sum(jnp.where(occ_match, occ_irrep[None, :], 0), axis=1)
    vir_lookup = jnp.sum(jnp.where(vir_match, slab_labels[None, :], 0), axis=1)
    col_labels = jnp.bitwise_xor(occ_lookup, vir_lookup)
    keep = row_labels[:, None] == col_labels[None, :]
    cycle = jnp.where(keep, sums, jnp.zeros_like(sums))
    return (ladder, cycle)


def solution(mesh):
    in_specs = (P("int", None), P("int", "amp"), P("int", "amp", None), P(), P())
    out_specs = (P("int", "amp"), P("int", "amp"))
    return jax.shard_map(
        per_device, mesh=mesh, in_specs=in_specs, out_specs=out_specs, check_vma=False
    )
```

```python
import jax
import jax.numpy as jnp
from jax import lax
from jax.experimental import pallas as pl
from jax.experimental.pallas import tpu as pltpu
from jax.sharding import PartitionSpec as P

F32 = jnp.float32
BF16 = jnp.bfloat16
MESH = pl.DeviceIdType.MESH

INT = 8
ROW = 8
COL = 4
WIDTHS = (800, 400, 400)
STARTS = (0, 800, 1200)
RIGHT, LEFT = 0, 1


def iota(shape, dim):
    return lax.broadcasted_iota(jnp.int32, shape, dim)


def split(x):
    high = x.astype(BF16)
    return high, (x - high.astype(F32)).astype(BF16)


def mm(a, b):
    return jnp.dot(a, b, preferred_element_type=F32)


def mm_nt(a, b):
    return lax.dot_general(a, b, (((1,), (1,)), ((), ())), preferred_element_type=F32)


def one_hot(match):
    return jnp.where(match, 1.0, 0.0).astype(BF16)


def body(
    amp_hbm, slab_hbm, w_hbm, occ_ref, vir_ref,
    lad_hbm, sum_ref,
    amp_ref, w_ref, lad_ref, slab, a3, acc0, acc1, acc2, table, s_buf, t_buf, u_buf, v_buf,
    wg, wpad, whi, wlo, msg, rcv, ct, rs, zs, zr, ys, yr, mask,
    in_sem, out_sem, ag_send, ag_recv, s_sem, u_sem, w_send, w_recv, a_send, a_recv, r_send, r_recv, z_sem, y_sem,
):
    d = lax.axis_index("amp")
    z = lax.axis_index("int")
    y = d // ROW
    xc = lax.rem(d, ROW)
    accs = (acc0, acc1, acc2)

    def around(step):
        return lax.rem(z + step + INT, INT)

    def in_row(j):
        return {"amp": y * ROW + lax.rem(xc + j, ROW), "int": z}

    def in_col(j):
        return {"amp": lax.rem(y + j, COL) * ROW + xc, "int": z}

    def in_stack(j):
        return {"amp": d, "int": lax.rem(z + j, INT)}

    barrier = pltpu.get_barrier_semaphore()

    @pl.loop(1, 8)
    def _(j):
        pl.semaphore_signal(barrier, inc=1, device_id=in_row(j), device_id_type=MESH)
        pl.semaphore_signal(barrier, inc=1, device_id=in_stack(j), device_id_type=MESH)

    @pl.loop(1, COL)
    def _(j):
        pl.semaphore_signal(barrier, inc=1, device_id=in_col(j), device_id_type=MESH)

    load_amp = pltpu.make_async_copy(amp_hbm, amp_ref, in_sem.at[0])
    load_slab = pltpu.make_async_copy(slab_hbm, slab.at[z], in_sem.at[1])
    load_w = pltpu.make_async_copy(w_hbm, w_ref, in_sem.at[2])
    load_amp.start()
    load_slab.start()
    load_w.start()

    def place(c, h):
        half = WIDTHS[c] // 2
        return pl.ds(STARTS[c] + half * h, half)

    def piece(way, c, j, h):
        hop = 1 if way == RIGHT else -1
        part = slab.at[around(-hop * (j - 1)), place(c, h), :]
        k = ((way * 3 + c) * 4 + (j - 1)) * 2 + h
        return pltpu.make_async_remote_copy(
            src_ref=part, dst_ref=part, send_sem=ag_send.at[k], recv_sem=ag_recv.at[k],
            device_id={"amp": d, "int": around(hop)}, device_id_type=MESH,
        )

    started = []

    def launch(way, c, j, h):
        copy = piece(way, c, j, h)
        copy.start()
        started.append(copy)

    def arrived(way, c, j, h):
        hop = 1 if way == RIGHT else -1
        part = slab.at[around(-hop * j), place(c, h), :]
        k = ((way * 3 + c) * 4 + (j - 1)) * 2 + h
        pltpu.make_async_copy(part, part, ag_recv.at[k]).wait()

    def begin(c):
        for h in range(2):
            for way in (RIGHT, LEFT):
                launch(way, c, 1, h)

    def event(c, j, h):
        for way in (RIGHT, LEFT):
            arrived(way, c, j, h)
            if j < 3 or h == way:
                launch(way, c, j + 1, h)

    def last(c):
        arrived(RIGHT, c, 4, 0)
        arrived(LEFT, c, 4, 1)

    def process(c, step):
        origin = around(step)
        a_block = a3[origin]
        tiles = ((0, 512), (512, 288)) if c == 0 else ((0, 400),)
        for col, n in tiles:
            high, low = split(slab[origin, STARTS[c] + col : STARTS[c] + col + n, :])
            part = mm_nt(a_block, jnp.concatenate([high, high, low], axis=1))
            if step == 0:
                accs[c][:, col : col + n] = part
            else:
                accs[c][:, col : col + n] += part

    load_amp.wait()
    here = pl.ds(pl.multiple_of(xc * 128, 128), 128)
    r, c = iota((256, 192), 0), iota((256, 192), 1)
    pick = one_hot((c == 96 * ((r >> 4) & 1) + 12 * (r >> 5) + (r & 15)) & ((r & 15) < 12))
    high, low = split(amp_ref[:, here])
    s_buf[...] = (mm(pick, high) + mm(pick, low)).reshape(INT, 32, 128)
    load_slab.wait()
    pl.semaphore_wait(barrier, 7 + 7 + 3)

    @pl.loop(1, INT)
    def _(j):
        up = lax.rem(z + j, INT)
        pltpu.make_async_remote_copy(
            src_ref=s_buf.at[up], dst_ref=t_buf.at[z], send_sem=s_sem.at[0], recv_sem=s_sem.at[1],
            device_id=in_stack(j), device_id_type=MESH,
        ).start()

    begin(0)
    t_buf[z] = s_buf[z]

    load_w.wait()
    for k in range(12):
        wg[y, 25 * k : 25 * k + 25, :] = w_ref[k]
    wg[y, 300:304, :] = jnp.zeros((4, 1024), F32)

    def w_piece(way, h, hop_from):
        hop = 1 if way == RIGHT else 3
        part = wg.at[lax.rem(y + (4 - hop) * hop_from, COL), pl.ds(152 * h, 152), :]
        k = way * 3 + (2 if hop_from else h)
        return pltpu.make_async_remote_copy(
            src_ref=part, dst_ref=part, send_sem=w_send.at[k], recv_sem=w_recv.at[k],
            device_id=in_col(hop), device_id_type=MESH,
        )

    def w_arrived(way, h, hops):
        hop = 1 if way == RIGHT else 3
        part = wg.at[lax.rem(y + (4 - hop) * hops, COL), pl.ds(152 * h, 152), :]
        pltpu.make_async_copy(part, part, w_recv.at[way * 3 + (2 if hops == 2 else h)]).wait()

    def w_launch(*which):
        copy = w_piece(*which)
        copy.start()
        started.append(copy)

    w_launch(RIGHT, 0, 0)
    w_launch(LEFT, 1, 0)
    w_launch(RIGHT, 1, 0)
    w_launch(LEFT, 0, 0)

    seven = pl.ds(0, 7)
    pltpu.make_async_copy(s_buf.at[seven], t_buf.at[seven], s_sem.at[1]).wait()
    r, c = iota((192, 256), 0), iota((192, 256), 1)
    pick = one_hot(c == 32 * ((r >> 1) & 7) + 16 * (r & 1) + (r >> 4))
    high, low = split(t_buf[...].reshape(256, 128))
    u_buf[...] = mm(pick, high) + mm(pick, low)

    @pl.loop(1, ROW)
    def _(j):
        pltpu.make_async_remote_copy(
            src_ref=u_buf, dst_ref=v_buf.at[xc], send_sem=u_sem.at[0], recv_sem=u_sem.at[1],
            device_id=in_row(j), device_id_type=MESH,
        ).start()

    v_buf[xc] = u_buf[...]

    r, c = iota((400, 512), 0), iota((400, 512), 1)
    table[...] = one_hot((r == 200 * (c >> 8) + 25 * ((c >> 5) & 7) + (c & 31)) & ((c & 31) < 25))

    sub, lane = iota((32, 128), 0), iota((32, 128), 1)
    row_label = jnp.where(lane < 64, occ_ref[2 * z], occ_ref[2 * z + 1])
    col_label = jnp.zeros((32, 128), jnp.int32) + occ_ref[d // 2]
    first = 32 * lax.rem(d, 2)

    def label_step(b, both):
        rows, cols = both
        rows = jnp.where((lane & 63) == b, rows ^ vir_ref[b], rows)
        cols = jnp.where(sub + first == b, cols ^ vir_ref[b], cols)
        return rows, cols

    row_label, col_label = lax.fori_loop(0, 64, label_step, (row_label, col_label))
    mask[...] = jnp.where(row_label == col_label, 1.0, 0.0).astype(F32)

    for o in range(INT):
        high, low = split(amp_ref[:, 128 * o : 128 * o + 128])
        a3[o, :192, 0:128] = high
        a3[o, :192, 128:256] = low
        a3[o, :192, 256:384] = high

    wpad[...] = jnp.zeros_like(wpad)

    def w_step(block):
        for k in range(12):
            wpad[32 * k : 32 * k + 25, :] = wg[block, 25 * k : 25 * k + 25, :]
        into = block // 2
        lanes = lax.rem(block, 2) * 384

        @pl.loop(0, 8)
        def _(i):
            at = pl.ds(pl.multiple_of(i * 128, 128), 128)
            for k4 in range(3):
                high, low = split(wpad[128 * k4 : 128 * k4 + 128, at].T)
                to = pl.ds(pl.multiple_of(lanes + 128 * k4, 128), 128)
                whi[into, at, to] = high
                wlo[into, at, to] = low

    event(0, 1, 0)
    w_step(y)
    event(0, 1, 1)
    event(0, 2, 0)
    pltpu.make_async_copy(v_buf.at[seven], v_buf.at[seven], u_sem.at[1]).wait()

    @pl.loop(0, INT)
    def _(o):
        high, low = split(v_buf[o])
        a3[o, 192:, 0:128] = high
        a3[o, 192:, 128:256] = low
        a3[o, 192:, 256:384] = high

    w_arrived(RIGHT, 0, 1)
    w_launch(RIGHT, 0, 1)
    w_arrived(LEFT, 1, 1)
    w_launch(LEFT, 1, 1)
    process(0, 0)
    process(0, -1)
    event(0, 2, 1)
    process(0, 1)
    process(0, -2)
    event(0, 3, 0)
    begin(1)
    process(0, 2)
    event(0, 3, 1)
    process(0, -3)
    process(0, 3)
    last(0)
    process(0, 4)

    def regroup(a, half):
        source = acc0[192:, 400 * half : 400 * half + 400] if a == 0 else accs[1 + half][192:, :]
        high, low = split(source)
        spaced = mm(high, table[...]) + mm(low, table[...])
        lane = iota((16, 128), 1)
        even = (lane & 32) == 0
        lower = (lane & 64) == 0
        for t in range(4):
            for k4 in range(3):
                x = [spaced[(4 * k4 + q) * 16 : (4 * k4 + q) * 16 + 16, 128 * t : 128 * t + 128] for q in range(4)]
                v = [None] * 4
                for q in (0, 2):
                    v[q] = jnp.where(even, x[q], pltpu.roll(x[q + 1], 32, 1))
                    v[q + 1] = jnp.where(even, pltpu.roll(x[q], 96, 1), x[q + 1])
                o = [None] * 4
                for q in (0, 1):
                    o[q] = jnp.where(lower, v[q], pltpu.roll(v[q + 2], 64, 1))
                    o[q + 2] = jnp.where(lower, pltpu.roll(v[q], 64, 1), v[q + 2])
                at = 384 * (t // 2) + 128 * k4
                for s in range(4):
                    msg[a, half, 4 * (t % 2) + s, :, at : at + 128] = o[s]

        @pl.loop(1, ROW)
        def _(j):
            to = lax.rem(xc + j, ROW)
            pltpu.make_async_remote_copy(
                src_ref=msg.at[a, half, to], dst_ref=rcv.at[a, half, xc],
                send_sem=a_send.at[2 * a + half], recv_sem=a_recv.at[2 * a + half],
                device_id=in_row(j), device_id_type=MESH,
            ).start()

        rcv[a, half, xc] = msg[a, half, xc]

    def contract(a, half):
        pltpu.make_async_copy(
            msg.at[a, half, seven], rcv.at[a, half, seven], a_recv.at[2 * a + half]
        ).wait()
        r, c = iota((128, 128), 0), iota((128, 128), 1)
        pick = one_hot(c == (r & 7) * 16 + 2 * (r >> 4) + ((r >> 3) & 1))
        high, low = split(rcv[a, half].reshape(128, 768))
        high = mm(pick, high).astype(BF16)
        low = mm(pick, low).astype(BF16)
        both = jnp.concatenate([high, low], axis=0)

        @pl.loop(0, COL)
        def _(q):
            at = pl.ds(pl.multiple_of(q * 256, 256), 256)
            part = mm_nt(whi[half, at, :], both)
            part = part[:, :128] + (part[:, 128:] + mm_nt(wlo[half, at, :], high))
            part = part.reshape(ROW, 32, 128)
            if half == 0:
                ct[a, :, q] = part
            else:
                ct[a, :, q] += part

        if half == 1:
            @pl.loop(1, ROW)
            def _(j):
                to = lax.rem(xc + j, ROW)
                pltpu.make_async_remote_copy(
                    src_ref=ct.at[a, to], dst_ref=rs.at[a, xc], send_sem=r_send.at[a], recv_sem=r_recv.at[a],
                    device_id=in_row(j), device_id_type=MESH,
                ).start()

            rs[a, xc] = ct[a, xc]

    def narrow(a):
        pltpu.make_async_copy(ct.at[a, seven], rs.at[a, seven], r_recv.at[a]).wait()
        total = rs[a, 0]
        for n in range(1, ROW):
            total += rs[a, n]
        zs[:, 16 * a : 16 * a + 16, :] = total.reshape(128, 128).T.reshape(INT, 16, 128)

    def w_rest(way, halves):
        for h in halves:
            w_arrived(way, h, 1)

    regroup(0, 0)
    regroup(0, 1)
    event(1, 1, 0)
    lad_ref[:, 0:800] = acc0[:192, :]
    event(1, 1, 1)
    store_0 = pltpu.make_async_copy(lad_ref.at[:, pl.ds(0, 768)], lad_hbm.at[:, pl.ds(0, 768)], out_sem.at[0])
    store_0.start()
    process(1, 0)
    process(1, -1)
    event(1, 2, 0)
    w_rest(RIGHT, (1,))
    w_step(lax.rem(y + 3, COL))
    event(1, 2, 1)
    begin(2)
    w_rest(LEFT, (0,))
    w_step(lax.rem(y + 1, COL))
    event(1, 3, 0)
    process(1, 1)
    process(1, -2)
    event(1, 3, 1)
    process(1, 2)
    process(1, -3)
    process(1, 3)
    last(1)
    process(1, 4)
    regroup(1, 0)
    event(2, 1, 0)
    w_arrived(RIGHT, 0, 2)
    w_arrived(LEFT, 1, 2)
    w_step(lax.rem(y + 2, COL))
    event(2, 1, 1)
    contract(0, 0)
    event(2, 2, 0)
    contract(0, 1)
    event(2, 2, 1)
    process(2, 0)
    process(2, -1)
    process(2, 1)
    event(2, 3, 0)
    contract(1, 0)
    event(2, 3, 1)
    process(2, -2)
    process(2, 2)
    process(2, -3)
    process(2, 3)
    last(2)
    process(2, 4)
    regroup(1, 1)
    lad_ref[:, 800:1200] = acc1[:192, :]
    lad_ref[:, 1200:1600] = acc2[:192, :]
    store_1 = pltpu.make_async_copy(lad_ref.at[:, pl.ds(768, 832)], lad_hbm.at[:, pl.ds(768, 832)], out_sem.at[1])
    store_1.start()
    narrow(0)
    contract(1, 1)
    narrow(1)

    @pl.loop(1, INT)
    def _(j):
        up = lax.rem(z + j, INT)
        pltpu.make_async_remote_copy(
            src_ref=zs.at[up], dst_ref=zr.at[z], send_sem=z_sem.at[0], recv_sem=z_sem.at[1],
            device_id=in_stack(j), device_id_type=MESH,
        ).start()

    zr[z] = zs[z]
    pltpu.make_async_copy(zs.at[seven], zr.at[seven], z_sem.at[1]).wait()
    total = zr[0]
    for n in range(1, INT):
        total += zr[n]
    ys[...] = total

    @pl.loop(1, COL)
    def _(j):
        pltpu.make_async_remote_copy(
            src_ref=ys, dst_ref=yr.at[y], send_sem=y_sem.at[0], recv_sem=y_sem.at[1],
            device_id=in_col(j), device_id_type=MESH,
        ).start()

    yr[y] = total
    three = pl.ds(0, 3)
    pltpu.make_async_copy(yr.at[three], yr.at[three], y_sem.at[1]).wait()
    exact = dict(precision=lax.Precision.HIGHEST, preferred_element_type=F32)
    nt = (((1,), (1,)), ((), ()))
    r, c = iota((32, 128), 0), iota((32, 128), 1)
    mine = jnp.where(c == 32 * y + r, 1.0, 0.0).astype(F32)
    kept = lax.dot_general(mine, yr[...].reshape(128, 128), nt, **exact)
    r, c = iota((128, 128), 0), iota((128, 128), 1)
    order = (r == 32 * ((c >> 4) & 3) + 16 * (c & 1) + 8 * (c >> 6) + ((c >> 1) & 7))
    kept = jnp.dot(kept, jnp.where(order, 1.0, 0.0).astype(F32), **exact)
    sum_ref[...] = jnp.where(mask[...] > 0.5, kept, jnp.zeros_like(kept))

    for copy in started:
        copy.wait_send()
    pltpu.make_async_copy(s_buf.at[seven], t_buf.at[seven], s_sem.at[0]).wait()
    pltpu.make_async_copy(v_buf.at[seven], v_buf.at[seven], u_sem.at[0]).wait()
    for a in range(2):
        for half in range(2):
            pltpu.make_async_copy(
                msg.at[a, half, seven], rcv.at[a, half, seven], a_send.at[2 * a + half]
            ).wait()
        pltpu.make_async_copy(ct.at[a, seven], rs.at[a, seven], r_send.at[a]).wait()
    pltpu.make_async_copy(zs.at[seven], zr.at[seven], z_sem.at[0]).wait()
    pltpu.make_async_copy(yr.at[three], yr.at[three], y_sem.at[0]).wait()
    store_0.wait()
    store_1.wait()


def per_device(amplitudes, slab_integrals, cycle_integrals, occ_irrep, vir_irrep):
    vmem = pl.BlockSpec(memory_space=pltpu.VMEM)
    smem = pl.BlockSpec(memory_space=pltpu.SMEM)
    anywhere = pl.BlockSpec(memory_space=pl.ANY)
    dma = pltpu.SemaphoreType.DMA
    ladder, sums = pl.pallas_call(
        body,
        out_shape=(
            jax.ShapeDtypeStruct((192, 1600), F32),
            jax.ShapeDtypeStruct((32, 128), F32),
        ),
        in_specs=[anywhere] * 3 + [smem] * 2,
        out_specs=(anywhere, vmem),
        scratch_shapes=[
            pltpu.VMEM((192, 1024), F32),
            pltpu.VMEM((12, 25, 1024), F32),
            pltpu.VMEM((192, 1600), F32),
            pltpu.VMEM((INT, 1600, 128), F32),
            pltpu.VMEM((INT, 384, 384), BF16),
            pltpu.VMEM((384, 800), F32),
            pltpu.VMEM((384, 400), F32),
            pltpu.VMEM((384, 400), F32),
            pltpu.VMEM((400, 512), BF16),
            pltpu.VMEM((INT, 32, 128), F32),
            pltpu.VMEM((INT, 32, 128), F32),
            pltpu.VMEM((192, 128), F32),
            pltpu.VMEM((INT, 192, 128), F32),
            pltpu.VMEM((COL, 304, 1024), F32),
            pltpu.VMEM((384, 1024), F32),
            pltpu.VMEM((2, 1024, 768), BF16),
            pltpu.VMEM((2, 1024, 768), BF16),
            pltpu.VMEM((2, 2, ROW, 16, 768), F32),
            pltpu.VMEM((2, 2, ROW, 16, 768), F32),
            pltpu.VMEM((2, ROW, COL, 32, 128), F32),
            pltpu.VMEM((2, ROW, COL, 32, 128), F32),
            pltpu.VMEM((INT, 32, 128), F32),
            pltpu.VMEM((INT, 32, 128), F32),
            pltpu.VMEM((32, 128), F32),
            pltpu.VMEM((COL, 32, 128), F32),
            pltpu.VMEM((32, 128), F32),
            dma((3,)),
            dma((2,)),
            dma((48,)),
            dma((48,)),
            dma((2,)),
            dma((2,)),
            dma((6,)),
            dma((6,)),
            dma((4,)),
            dma((4,)),
            dma((2,)),
            dma((2,)),
            dma((2,)),
            dma((2,)),
        ],
        compiler_params=pltpu.CompilerParams(
            collective_id=0, has_side_effects=True, vmem_limit_bytes=58 * 1024 * 1024
        ),
        cost_estimate=pl.CostEstimate(flops=8_000_000_000, bytes_accessed=8_000_000, transcendentals=0),
    )(amplitudes, slab_integrals.T, cycle_integrals, occ_irrep, vir_irrep)
    return ladder, sums.T


def solution(mesh):
    in_specs = (P("int", None), P("int", "amp"), P("int", "amp", None), P(), P())
    out_specs = (P("int", "amp"), P("int", "amp"))
    return jax.shard_map(
        per_device, mesh=mesh, in_specs=in_specs, out_specs=out_specs, check_vma=False
    )
```

```python
import jax
import jax.numpy as jnp
from jax import lax
from jax.experimental import pallas as pl
from jax.experimental.pallas import tpu as pltpu
from jax.sharding import PartitionSpec as P

F32 = jnp.float32
BF16 = jnp.bfloat16
MESH = pl.DeviceIdType.MESH

INT = 8
ROW = 8
COL = 4
PLANE = ROW * COL
WIDTHS = (800, 400, 400)
STARTS = (0, 800, 1200)
PIECES = tuple(
    tuple((start + width * q // 4 // 8 * 8, (width * (q + 1) // 4 // 8 - width * q // 4 // 8) * 8) for q in range(4))
    for start, width in zip(STARTS, WIDTHS)
)
RIGHT, LEFT = 0, 1


def iota(shape, dim):
    return lax.broadcasted_iota(jnp.int32, shape, dim)


def split(x):
    high = x.astype(BF16)
    return high, (x - high.astype(F32)).astype(BF16)


def mm(a, b):
    return jnp.dot(a, b, preferred_element_type=F32)


def mm_nt(a, b):
    return lax.dot_general(a, b, (((1,), (1,)), ((), ())), preferred_element_type=F32)


def one_hot(match):
    return jnp.where(match, 1.0, 0.0).astype(BF16)


def body(
    amp_hbm, slab_hbm, w_hbm, occ_ref, vir_ref,
    lad_hbm, sum_ref,
    amp_ref, w_ref, lad_ref, slab, a3, acc0, acc1, acc2, table, s_buf, t_buf, u_buf, v_buf,
    wg, wpad, whi, wlo, msg, rcv, ct, rs, zs, zr, mask,
    in_sem, out_sem, ag_send, ag_recv, s_sem, u_sem, w_send, w_recv, a_send, a_recv, r_send, r_recv, z_sem,
):
    d = lax.axis_index("amp")
    z = lax.axis_index("int")
    y = d // ROW
    xc = lax.rem(d, ROW)
    accs = (acc0, acc1, acc2)

    def around(step):
        return lax.rem(z + step + INT, INT)

    def in_row(j):
        return {"amp": y * ROW + lax.rem(xc + j, ROW), "int": z}

    def in_col(j):
        return {"amp": lax.rem(y + j, COL) * ROW + xc, "int": z}

    def in_stack(j):
        return {"amp": d, "int": lax.rem(z + j, INT)}

    barrier = pltpu.get_barrier_semaphore()

    @pl.loop(1, PLANE)
    def _(j):
        pl.semaphore_signal(barrier, inc=1, device_id={"amp": lax.rem(d + j, PLANE), "int": z}, device_id_type=MESH)

    @pl.loop(1, INT)
    def _(j):
        pl.semaphore_signal(barrier, inc=1, device_id=in_stack(j), device_id_type=MESH)

    load_amp = pltpu.make_async_copy(amp_hbm, amp_ref, in_sem.at[0])
    load_slab = pltpu.make_async_copy(slab_hbm, slab.at[z], in_sem.at[1])
    load_w = pltpu.make_async_copy(w_hbm, w_ref, in_sem.at[2])
    load_amp.start()
    load_slab.start()
    load_w.start()

    def place(c, q):
        return pl.ds(*PIECES[c][q])

    def piece(way, c, j, q):
        hop = 1 if way == RIGHT else -1
        part = slab.at[around(-hop * (j - 1)), place(c, q), :]
        k = ((way * 3 + c) * 4 + (j - 1)) * 4 + q
        return pltpu.make_async_remote_copy(
            src_ref=part, dst_ref=part, send_sem=ag_send.at[k], recv_sem=ag_recv.at[k],
            device_id={"amp": d, "int": around(hop)}, device_id_type=MESH,
        )

    started = []

    def launch(way, c, j, q):
        copy = piece(way, c, j, q)
        copy.start()
        started.append(copy)

    def arrived(way, c, j, q):
        hop = 1 if way == RIGHT else -1
        part = slab.at[around(-hop * j), place(c, q), :]
        k = ((way * 3 + c) * 4 + (j - 1)) * 4 + q
        pltpu.make_async_copy(part, part, ag_recv.at[k]).wait()

    order = ((RIGHT, 0), (LEFT, 3), (RIGHT, 1), (LEFT, 2)), ((RIGHT, 2), (LEFT, 1), (RIGHT, 3), (LEFT, 0))

    def begin(c):
        for way, q in order[0] + order[1]:
            launch(way, c, 1, q)

    def event(c, j, g):
        for way, q in order[g]:
            arrived(way, c, j, q)
            if j < 3 or g == 0:
                launch(way, c, j + 1, q)

    def last(c):
        for way, q in order[0]:
            arrived(way, c, 4, q)

    def process(c, step):
        origin = around(step)
        a_block = a3[origin]
        tiles = ((0, 512), (512, 288)) if c == 0 else ((0, 400),)
        for col, n in tiles:
            high, low = split(slab[origin, STARTS[c] + col : STARTS[c] + col + n, :])
            part = mm_nt(a_block, jnp.concatenate([high, high, low], axis=1))
            if step == 0:
                accs[c][:, col : col + n] = part
            else:
                accs[c][:, col : col + n] += part

    load_amp.wait()
    here = pl.ds(pl.multiple_of(xc * 128, 128), 128)
    r, c = iota((256, 192), 0), iota((256, 192), 1)
    pick = one_hot((c == 96 * ((r >> 4) & 1) + 12 * (r >> 5) + (r & 15)) & ((r & 15) < 12))
    high, low = split(amp_ref[:, here])
    s_buf[...] = (mm(pick, high) + mm(pick, low)).reshape(INT, 32, 128)
    load_slab.wait()
    pl.semaphore_wait(barrier, PLANE - 1 + INT - 1)

    @pl.loop(1, INT)
    def _(j):
        up = lax.rem(z + j, INT)
        pltpu.make_async_remote_copy(
            src_ref=s_buf.at[up], dst_ref=t_buf.at[z], send_sem=s_sem.at[0], recv_sem=s_sem.at[1],
            device_id=in_stack(j), device_id_type=MESH,
        ).start()

    begin(0)
    t_buf[z] = s_buf[z]

    load_w.wait()
    for k in range(12):
        wg[y, 25 * k : 25 * k + 25, :] = w_ref[k]
    wg[y, 300:304, :] = jnp.zeros((4, 1024), F32)

    def w_piece(way, h, hop_from):
        hop = 1 if way == RIGHT else 3
        part = wg.at[lax.rem(y + (4 - hop) * hop_from, COL), pl.ds(152 * h, 152), :]
        k = way * 3 + (2 if hop_from else h)
        return pltpu.make_async_remote_copy(
            src_ref=part, dst_ref=part, send_sem=w_send.at[k], recv_sem=w_recv.at[k],
            device_id=in_col(hop), device_id_type=MESH,
        )

    def w_arrived(way, h, hops):
        hop = 1 if way == RIGHT else 3
        part = wg.at[lax.rem(y + (4 - hop) * hops, COL), pl.ds(152 * h, 152), :]
        pltpu.make_async_copy(part, part, w_recv.at[way * 3 + (2 if hops == 2 else h)]).wait()

    def w_launch(*which):
        copy = w_piece(*which)
        copy.start()
        started.append(copy)

    w_launch(RIGHT, 0, 0)
    w_launch(LEFT, 1, 0)
    w_launch(RIGHT, 1, 0)
    w_launch(LEFT, 0, 0)

    seven = pl.ds(0, 7)

    r, c = iota((400, 512), 0), iota((400, 512), 1)
    table[...] = one_hot((r == 200 * (c >> 8) + 25 * ((c >> 5) & 7) + (c & 31)) & ((c & 31) < 25))

    sub, lane = iota((32, 128), 0), iota((32, 128), 1)
    row_label = jnp.where(lane < 64, occ_ref[2 * z], occ_ref[2 * z + 1])
    col_label = jnp.zeros((32, 128), jnp.int32) + occ_ref[d // 2]
    first = 32 * lax.rem(d, 2)

    def label_step(b, both):
        rows, cols = both
        rows = jnp.where((lane & 63) == b, rows ^ vir_ref[b], rows)
        cols = jnp.where(sub + first == b, cols ^ vir_ref[b], cols)
        return rows, cols

    row_label, col_label = lax.fori_loop(0, 64, label_step, (row_label, col_label))
    mask[...] = jnp.where(row_label == col_label, 1.0, 0.0).astype(F32)

    for o in range(INT):
        high, low = split(amp_ref[:, 128 * o : 128 * o + 128])
        a3[o, :192, 0:128] = high
        a3[o, :192, 128:256] = low
        a3[o, :192, 256:384] = high

    wpad[...] = jnp.zeros_like(wpad)

    def w_step(block):
        for k in range(12):
            wpad[32 * k : 32 * k + 25, :] = wg[block, 25 * k : 25 * k + 25, :]
        into = block // 2
        lanes = lax.rem(block, 2) * 384

        @pl.loop(0, 8)
        def _(i):
            at = pl.ds(pl.multiple_of(i * 128, 128), 128)
            for k4 in range(3):
                high, low = split(wpad[128 * k4 : 128 * k4 + 128, at].T)
                to = pl.ds(pl.multiple_of(lanes + 128 * k4, 128), 128)
                whi[into, at, to] = high
                wlo[into, at, to] = low

    event(0, 1, 0)
    pltpu.make_async_copy(s_buf.at[seven], t_buf.at[seven], s_sem.at[1]).wait()
    r, c = iota((192, 256), 0), iota((192, 256), 1)
    pick = one_hot(c == 32 * ((r >> 1) & 7) + 16 * (r & 1) + (r >> 4))
    high, low = split(t_buf[...].reshape(256, 128))
    u_buf[...] = mm(pick, high) + mm(pick, low)

    @pl.loop(1, ROW)
    def _(j):
        pltpu.make_async_remote_copy(
            src_ref=u_buf, dst_ref=v_buf.at[xc], send_sem=u_sem.at[0], recv_sem=u_sem.at[1],
            device_id=in_row(j), device_id_type=MESH,
        ).start()

    v_buf[xc] = u_buf[...]
    event(0, 1, 1)
    w_step(y)
    event(0, 2, 0)
    event(0, 2, 1)
    w_arrived(RIGHT, 0, 1)
    w_launch(RIGHT, 0, 1)
    w_arrived(LEFT, 1, 1)
    w_launch(LEFT, 1, 1)
    pltpu.make_async_copy(v_buf.at[seven], v_buf.at[seven], u_sem.at[1]).wait()

    @pl.loop(0, INT)
    def _(o):
        high, low = split(v_buf[o])
        a3[o, 192:, 0:128] = high
        a3[o, 192:, 128:256] = low
        a3[o, 192:, 256:384] = high

    process(0, 0)
    process(0, -1)
    process(0, 1)
    event(0, 3, 0)
    begin(1)
    process(0, -2)
    process(0, 2)
    event(0, 3, 1)
    process(0, -3)
    process(0, 3)
    last(0)
    process(0, 4)

    def regroup(a, half):
        source = acc0[192:, 400 * half : 400 * half + 400] if a == 0 else accs[1 + half][192:, :]
        high, low = split(source)
        spaced = mm(high, table[...]) + mm(low, table[...])
        lane = iota((16, 128), 1)
        even = (lane & 32) == 0
        lower = (lane & 64) == 0
        for t in range(4):
            for k4 in range(3):
                x = [spaced[(4 * k4 + q) * 16 : (4 * k4 + q) * 16 + 16, 128 * t : 128 * t + 128] for q in range(4)]
                v = [None] * 4
                for q in (0, 2):
                    v[q] = jnp.where(even, x[q], pltpu.roll(x[q + 1], 32, 1))
                    v[q + 1] = jnp.where(even, pltpu.roll(x[q], 96, 1), x[q + 1])
                o = [None] * 4
                for q in (0, 1):
                    o[q] = jnp.where(lower, v[q], pltpu.roll(v[q + 2], 64, 1))
                    o[q + 2] = jnp.where(lower, pltpu.roll(v[q], 64, 1), v[q + 2])
                at = 384 * (t // 2) + 128 * k4
                for s in range(4):
                    msg[a, half, 4 * (t % 2) + s, :, at : at + 128] = o[s]

        @pl.loop(1, ROW)
        def _(j):
            to = lax.rem(xc + j, ROW)
            pltpu.make_async_remote_copy(
                src_ref=msg.at[a, half, to], dst_ref=rcv.at[a, half, xc],
                send_sem=a_send.at[2 * a + half], recv_sem=a_recv.at[2 * a + half],
                device_id=in_row(j), device_id_type=MESH,
            ).start()

        rcv[a, half, xc] = msg[a, half, xc]

    def contract(a, half):
        pltpu.make_async_copy(
            msg.at[a, half, seven], rcv.at[a, half, seven], a_recv.at[2 * a + half]
        ).wait()
        r, c = iota((128, 128), 0), iota((128, 128), 1)
        pick = one_hot(c == (r & 7) * 16 + 2 * (r >> 4) + ((r >> 3) & 1))
        high, low = split(rcv[a, half].reshape(128, 768))
        high = mm(pick, high).astype(BF16)
        low = mm(pick, low).astype(BF16)
        both = jnp.concatenate([high, low], axis=0)

        @pl.loop(0, COL)
        def _(q):
            to_row = lax.rem(y + q, COL)
            at = pl.ds(pl.multiple_of(to_row * 256, 256), 256)
            into = pl.ds(to_row * ROW, ROW)
            part = mm_nt(whi[half, at, :], both)
            part = part[:, :128] + (part[:, 128:] + mm_nt(wlo[half, at, :], high))
            part = part.reshape(ROW, 32, 128)
            if half == 0:
                ct[a, into] = part
            else:
                ct[a, into] += part

                @pl.loop(0, ROW)
                def _(n):
                    to = to_row * ROW + lax.rem(xc + n, ROW)

                    @pl.when(to != d)
                    def _():
                        pltpu.make_async_remote_copy(
                            src_ref=ct.at[a, to], dst_ref=rs.at[a, d], send_sem=r_send.at[a], recv_sem=r_recv.at[a],
                            device_id={"amp": to, "int": z}, device_id_type=MESH,
                        ).start()

        if half == 1:
            rs[a, d] = ct[a, d]

    others = pl.ds(0, PLANE - 1)

    def narrow(a):
        pltpu.make_async_copy(ct.at[a, others], rs.at[a, others], r_recv.at[a]).wait()
        rows = []
        for row in range(COL):
            total = rs[a, row * ROW]
            for n in range(1, ROW):
                total += rs[a, row * ROW + n]
            rows.append(total)
        zs[:, 16 * a : 16 * a + 16, :] = jnp.concatenate(rows, axis=0).T.reshape(INT, 16, 128)

    def w_rest(way, halves):
        for h in halves:
            w_arrived(way, h, 1)

    regroup(0, 0)
    regroup(0, 1)
    w_rest(RIGHT, (1,))
    w_step(lax.rem(y + 3, COL))
    event(1, 1, 0)
    lad_ref[:, 0:800] = acc0[:192, :]
    store_0 = pltpu.make_async_copy(lad_ref.at[:, pl.ds(0, 768)], lad_hbm.at[:, pl.ds(0, 768)], out_sem.at[0])
    store_0.start()
    event(1, 1, 1)
    w_rest(LEFT, (0,))
    w_step(lax.rem(y + 1, COL))
    event(1, 2, 0)
    process(1, 0)
    process(1, -1)
    event(1, 2, 1)
    w_arrived(RIGHT, 0, 2)
    w_arrived(LEFT, 1, 2)
    w_step(lax.rem(y + 2, COL))
    event(1, 3, 0)
    begin(2)
    contract(0, 0)
    event(1, 3, 1)
    contract(0, 1)
    process(1, 1)
    process(1, -2)
    process(1, 2)
    process(1, -3)
    process(1, 3)
    last(1)
    process(1, 4)
    regroup(1, 0)
    event(2, 1, 0)
    event(2, 1, 1)
    process(2, 0)
    event(2, 2, 0)
    process(2, -1)
    event(2, 2, 1)
    process(2, 1)
    event(2, 3, 0)
    contract(1, 0)
    event(2, 3, 1)
    process(2, -2)
    process(2, 2)
    process(2, -3)
    process(2, 3)
    last(2)
    process(2, 4)
    regroup(1, 1)
    lad_ref[:, 800:1200] = acc1[:192, :]
    lad_ref[:, 1200:1600] = acc2[:192, :]
    store_1 = pltpu.make_async_copy(lad_ref.at[:, pl.ds(768, 832)], lad_hbm.at[:, pl.ds(768, 832)], out_sem.at[1])
    store_1.start()
    narrow(0)
    contract(1, 1)
    narrow(1)

    @pl.loop(1, INT)
    def _(j):
        up = lax.rem(z + j, INT)
        pltpu.make_async_remote_copy(
            src_ref=zs.at[up], dst_ref=zr.at[z], send_sem=z_sem.at[0], recv_sem=z_sem.at[1],
            device_id=in_stack(j), device_id_type=MESH,
        ).start()

    zr[z] = zs[z]
    pltpu.make_async_copy(zs.at[seven], zr.at[seven], z_sem.at[1]).wait()
    total = zr[0]
    for n in range(1, INT):
        total += zr[n]
    total = total.T
    m, r = iota((32, 128), 0), iota((32, 128), 1)
    kept = jnp.zeros((32, 128), F32)
    for row in range(COL):
        match = ((m >> 3) & 1 == r >> 6) & (m >> 4 == r & 1) & (m & 7 == (r >> 1) & 7) & ((r >> 4) & 3 == row)
        kept += jnp.dot(
            total[32 * row : 32 * row + 32], jnp.where(match, 1.0, 0.0).astype(F32),
            precision=lax.Precision.HIGHEST, preferred_element_type=F32,
        )
    sum_ref[...] = jnp.where(mask[...] > 0.5, kept, jnp.zeros_like(kept))

    for copy in started:
        copy.wait_send()
    pltpu.make_async_copy(s_buf.at[seven], t_buf.at[seven], s_sem.at[0]).wait()
    pltpu.make_async_copy(v_buf.at[seven], v_buf.at[seven], u_sem.at[0]).wait()
    for a in range(2):
        for half in range(2):
            pltpu.make_async_copy(
                msg.at[a, half, seven], rcv.at[a, half, seven], a_send.at[2 * a + half]
            ).wait()
        pltpu.make_async_copy(ct.at[a, others], rs.at[a, others], r_send.at[a]).wait()
    pltpu.make_async_copy(zs.at[seven], zr.at[seven], z_sem.at[0]).wait()
    store_0.wait()
    store_1.wait()


def per_device(amplitudes, slab_integrals, cycle_integrals, occ_irrep, vir_irrep):
    vmem = pl.BlockSpec(memory_space=pltpu.VMEM)
    smem = pl.BlockSpec(memory_space=pltpu.SMEM)
    anywhere = pl.BlockSpec(memory_space=pl.ANY)
    dma = pltpu.SemaphoreType.DMA
    ladder, sums = pl.pallas_call(
        body,
        out_shape=(
            jax.ShapeDtypeStruct((192, 1600), F32),
            jax.ShapeDtypeStruct((32, 128), F32),
        ),
        in_specs=[anywhere] * 3 + [smem] * 2,
        out_specs=(anywhere, vmem),
        scratch_shapes=[
            pltpu.VMEM((192, 1024), F32),
            pltpu.VMEM((12, 25, 1024), F32),
            pltpu.VMEM((192, 1600), F32),
            pltpu.VMEM((INT, 1600, 128), F32),
            pltpu.VMEM((INT, 384, 384), BF16),
            pltpu.VMEM((384, 800), F32),
            pltpu.VMEM((384, 400), F32),
            pltpu.VMEM((384, 400), F32),
            pltpu.VMEM((400, 512), BF16),
            pltpu.VMEM((INT, 32, 128), F32),
            pltpu.VMEM((INT, 32, 128), F32),
            pltpu.VMEM((192, 128), F32),
            pltpu.VMEM((INT, 192, 128), F32),
            pltpu.VMEM((COL, 304, 1024), F32),
            pltpu.VMEM((384, 1024), F32),
            pltpu.VMEM((2, 1024, 768), BF16),
            pltpu.VMEM((2, 1024, 768), BF16),
            pltpu.VMEM((2, 2, ROW, 16, 768), F32),
            pltpu.VMEM((2, 2, ROW, 16, 768), F32),
            pltpu.VMEM((2, PLANE, 32, 128), F32),
            pltpu.VMEM((2, PLANE, 32, 128), F32),
            pltpu.VMEM((INT, 32, 128), F32),
            pltpu.VMEM((INT, 32, 128), F32),
            pltpu.VMEM((32, 128), F32),
            dma((3,)),
            dma((2,)),
            dma((96,)),
            dma((96,)),
            dma((2,)),
            dma((2,)),
            dma((6,)),
            dma((6,)),
            dma((4,)),
            dma((4,)),
            dma((2,)),
            dma((2,)),
            dma((2,)),
        ],
        compiler_params=pltpu.CompilerParams(
            collective_id=0, has_side_effects=True, vmem_limit_bytes=58 * 1024 * 1024
        ),
        cost_estimate=pl.CostEstimate(flops=8_000_000_000, bytes_accessed=8_000_000, transcendentals=0),
    )(amplitudes, slab_integrals.T, cycle_integrals, occ_irrep, vir_irrep)
    return ladder, sums.T


def solution(mesh):
    in_specs = (P("int", None), P("int", "amp"), P("int", "amp", None), P(), P())
    out_specs = (P("int", "amp"), P("int", "amp"))
    return jax.shard_map(
        per_device, mesh=mesh, in_specs=in_specs, out_specs=out_specs, check_vma=False
    )
```

```python
import jax
import jax.numpy as jnp
from jax import lax
from jax.experimental import pallas as pl
from jax.experimental.pallas import tpu as pltpu
from jax.sharding import PartitionSpec as P

F32 = jnp.float32
BF16 = jnp.bfloat16
MESH = pl.DeviceIdType.MESH

INT = 8
ROW = 8
COL = 4
PLANE = ROW * COL
WIDTHS = (800, 400, 400)
STARTS = (0, 800, 1200)
PIECES = tuple(
    tuple((start + width * q // 4 // 8 * 8, (width * (q + 1) // 4 // 8 - width * q // 4 // 8) * 8) for q in range(4))
    for start, width in zip(STARTS, WIDTHS)
)
RIGHT, LEFT = 0, 1


def iota(shape, dim):
    return lax.broadcasted_iota(jnp.int32, shape, dim)


def split(x):
    high = x.astype(BF16)
    return high, (x - high.astype(F32)).astype(BF16)


def mm(a, b):
    return jnp.dot(a, b, preferred_element_type=F32)


def mm_nt(a, b):
    return lax.dot_general(a, b, (((1,), (1,)), ((), ())), preferred_element_type=F32)


def one_hot(match):
    return jnp.where(match, 1.0, 0.0).astype(BF16)


def body(
    amp_hbm, slab_hbm, w_hbm, occ_ref, vir_ref,
    lad_hbm, sum_ref,
    amp_ref, w_ref, lad_ref, slab, a3, acc0, acc1, acc2, table, s_buf, t_buf, u_buf, v_buf,
    wg, wpad, whi, wlo, msg, rcv, ct, rs, zs, zr, mask,
    in_sem, out_sem, ag_send, ag_recv, s_sem, u_sem, w_send, w_recv, a_send, a_recv, r_send, r_recv, z_sem,
):
    d = lax.axis_index("amp")
    z = lax.axis_index("int")
    y = d // ROW
    xc = lax.rem(d, ROW)
    accs = (acc0, acc1, acc2)

    def around(step):
        return lax.rem(z + step + INT, INT)

    def in_row(j):
        return {"amp": y * ROW + lax.rem(xc + j, ROW), "int": z}

    def in_col(j):
        return {"amp": lax.rem(y + j, COL) * ROW + xc, "int": z}

    def in_stack(j):
        return {"amp": d, "int": lax.rem(z + j, INT)}

    barrier = pltpu.get_barrier_semaphore()

    for j in (1, INT - 1, 2, INT - 2, 3, INT - 3, 4):
        pl.semaphore_signal(barrier, inc=1, device_id=in_stack(j), device_id_type=MESH)
    for j in (1, COL - 1):
        pl.semaphore_signal(barrier, inc=1, device_id=in_col(j), device_id_type=MESH)

    @pl.loop(1, ROW)
    def _(j):
        pl.semaphore_signal(barrier, inc=1, device_id=in_row(j), device_id_type=MESH)

    load_amp = pltpu.make_async_copy(amp_hbm, amp_ref, in_sem.at[0])
    load_slab = pltpu.make_async_copy(slab_hbm, slab.at[z], in_sem.at[1])
    load_w = pltpu.make_async_copy(w_hbm, w_ref, in_sem.at[2])
    load_amp.start()
    load_slab.start()
    load_w.start()

    def place(c, q):
        return pl.ds(*PIECES[c][q])

    def piece(way, c, j, q):
        hop = 1 if way == RIGHT else -1
        part = slab.at[around(-hop * (j - 1)), place(c, q), :]
        source = slab_hbm.at[place(c, q), :] if j == 1 else part
        k = ((way * 3 + c) * 4 + (j - 1)) * 4 + q
        return pltpu.make_async_remote_copy(
            src_ref=source, dst_ref=part, send_sem=ag_send.at[k], recv_sem=ag_recv.at[k],
            device_id={"amp": d, "int": around(hop)}, device_id_type=MESH,
        )

    started = []

    def launch(way, c, j, q):
        copy = piece(way, c, j, q)
        copy.start()
        started.append(copy)

    def arrived(way, c, j, q):
        hop = 1 if way == RIGHT else -1
        part = slab.at[around(-hop * j), place(c, q), :]
        k = ((way * 3 + c) * 4 + (j - 1)) * 4 + q
        pltpu.make_async_copy(part, part, ag_recv.at[k]).wait()

    order = ((RIGHT, 0), (LEFT, 3), (RIGHT, 1), (LEFT, 2)), ((RIGHT, 2), (LEFT, 1), (RIGHT, 3), (LEFT, 0))

    def begin(c):
        for way, q in order[0] + order[1]:
            launch(way, c, 1, q)

    def event(c, j, g):
        for way, q in order[g]:
            arrived(way, c, j, q)
            if j < 3 or g == 0:
                launch(way, c, j + 1, q)

    def last(c):
        for way, q in order[0]:
            arrived(way, c, 4, q)

    def process(c, step):
        origin = around(step)
        a_block = a3[origin]
        tiles = ((0, 512), (512, 288)) if c == 0 else ((0, 400),)
        for col, n in tiles:
            high, low = split(slab[origin, STARTS[c] + col : STARTS[c] + col + n, :])
            part = mm_nt(a_block, jnp.concatenate([high, high, low], axis=1))
            if step == 0:
                accs[c][:, col : col + n] = part
            else:
                accs[c][:, col : col + n] += part

    load_amp.wait()
    here = pl.ds(pl.multiple_of(xc * 128, 128), 128)
    r, c = iota((256, 192), 0), iota((256, 192), 1)
    pick = one_hot((c == 96 * ((r >> 4) & 1) + 12 * (r >> 5) + (r & 15)) & ((r & 15) < 12))
    high, low = split(amp_ref[:, here])
    s_buf[...] = (mm(pick, high) + mm(pick, low)).reshape(INT, 32, 128)
    pl.semaphore_wait(barrier, INT - 1 + 2 + ROW - 1)

    @pl.loop(1, INT)
    def _(j):
        up = lax.rem(z + j, INT)
        pltpu.make_async_remote_copy(
            src_ref=s_buf.at[up], dst_ref=t_buf.at[z], send_sem=s_sem.at[0], recv_sem=s_sem.at[1],
            device_id=in_stack(j), device_id_type=MESH,
        ).start()

    begin(0)
    t_buf[z] = s_buf[z]

    load_w.wait()
    for k in range(12):
        wg[y, 25 * k : 25 * k + 25, :] = w_ref[k]
    wg[y, 300:304, :] = jnp.zeros((4, 1024), F32)

    def w_piece(way, h, hop_from):
        hop = 1 if way == RIGHT else 3
        part = wg.at[lax.rem(y + (4 - hop) * hop_from, COL), pl.ds(152 * h, 152), :]
        k = way * 3 + (2 if hop_from else h)
        return pltpu.make_async_remote_copy(
            src_ref=part, dst_ref=part, send_sem=w_send.at[k], recv_sem=w_recv.at[k],
            device_id=in_col(hop), device_id_type=MESH,
        )

    def w_arrived(way, h, hops):
        hop = 1 if way == RIGHT else 3
        part = wg.at[lax.rem(y + (4 - hop) * hops, COL), pl.ds(152 * h, 152), :]
        pltpu.make_async_copy(part, part, w_recv.at[way * 3 + (2 if hops == 2 else h)]).wait()

    def w_launch(*which):
        copy = w_piece(*which)
        copy.start()
        started.append(copy)

    w_launch(RIGHT, 0, 0)
    w_launch(LEFT, 1, 0)
    w_launch(RIGHT, 1, 0)
    w_launch(LEFT, 0, 0)

    seven = pl.ds(0, 7)

    r, c = iota((400, 512), 0), iota((400, 512), 1)
    table[...] = one_hot((r == 200 * (c >> 8) + 25 * ((c >> 5) & 7) + (c & 31)) & ((c & 31) < 25))

    def w_step(block):
        for k in range(12):
            wpad[32 * k : 32 * k + 25, :] = wg[block, 25 * k : 25 * k + 25, :]
        into = block // 2
        lanes = lax.rem(block, 2) * 384

        @pl.loop(0, 8)
        def _(i):
            at = pl.ds(pl.multiple_of(i * 128, 128), 128)
            for k4 in range(3):
                high, low = split(wpad[128 * k4 : 128 * k4 + 128, at].T)
                to = pl.ds(pl.multiple_of(lanes + 128 * k4, 128), 128)
                whi[into, at, to] = high
                wlo[into, at, to] = low

    event(0, 1, 0)
    pltpu.make_async_copy(s_buf.at[seven], t_buf.at[seven], s_sem.at[1]).wait()
    r, c = iota((192, 256), 0), iota((192, 256), 1)
    pick = one_hot(c == 32 * ((r >> 1) & 7) + 16 * (r & 1) + (r >> 4))
    high, low = split(t_buf[...].reshape(256, 128))
    u_buf[...] = mm(pick, high) + mm(pick, low)

    @pl.loop(1, ROW)
    def _(j):
        pltpu.make_async_remote_copy(
            src_ref=u_buf, dst_ref=v_buf.at[xc], send_sem=u_sem.at[0], recv_sem=u_sem.at[1],
            device_id=in_row(j), device_id_type=MESH,
        ).start()

    v_buf[xc] = u_buf[...]
    event(0, 1, 1)
    for o in range(INT):
        high, low = split(amp_ref[:, 128 * o : 128 * o + 128])
        a3[o, :192, 0:128] = high
        a3[o, :192, 128:256] = low
        a3[o, :192, 256:384] = high

    wpad[...] = jnp.zeros_like(wpad)
    event(0, 2, 0)
    w_step(y)
    event(0, 2, 1)
    w_arrived(RIGHT, 0, 1)
    w_launch(RIGHT, 0, 1)
    w_arrived(LEFT, 1, 1)
    w_launch(LEFT, 1, 1)
    pltpu.make_async_copy(v_buf.at[seven], v_buf.at[seven], u_sem.at[1]).wait()

    @pl.loop(0, INT)
    def _(o):
        high, low = split(v_buf[o])
        a3[o, 192:, 0:128] = high
        a3[o, 192:, 128:256] = low
        a3[o, 192:, 256:384] = high
    load_slab.wait()
    process(0, 0)
    process(0, -1)
    process(0, 1)
    event(0, 3, 0)
    begin(1)
    process(0, -2)
    process(0, 2)
    event(0, 3, 1)
    process(0, -3)
    process(0, 3)

    def regroup(a, half):
        source = acc0[192:, 400 * half : 400 * half + 400] if a == 0 else accs[1 + half][192:, :]
        high, low = split(source)
        spaced = mm(high, table[...]) + mm(low, table[...])
        lane = iota((16, 128), 1)
        even = (lane & 32) == 0
        lower = (lane & 64) == 0
        for t in range(4):
            for k4 in range(3):
                x = [spaced[(4 * k4 + q) * 16 : (4 * k4 + q) * 16 + 16, 128 * t : 128 * t + 128] for q in range(4)]
                v = [None] * 4
                for q in (0, 2):
                    v[q] = jnp.where(even, x[q], pltpu.roll(x[q + 1], 32, 1))
                    v[q + 1] = jnp.where(even, pltpu.roll(x[q], 96, 1), x[q + 1])
                o = [None] * 4
                for q in (0, 1):
                    o[q] = jnp.where(lower, v[q], pltpu.roll(v[q + 2], 64, 1))
                    o[q + 2] = jnp.where(lower, pltpu.roll(v[q], 64, 1), v[q + 2])
                at = 384 * (t // 2) + 128 * k4
                for s in range(4):
                    msg[a, half, 4 * (t % 2) + s, :, at : at + 128] = o[s]

        @pl.loop(1, ROW)
        def _(j):
            to = lax.rem(xc + j, ROW)
            pltpu.make_async_remote_copy(
                src_ref=msg.at[a, half, to], dst_ref=rcv.at[a, half, xc],
                send_sem=a_send.at[2 * a + half], recv_sem=a_recv.at[2 * a + half],
                device_id=in_row(j), device_id_type=MESH,
            ).start()

        rcv[a, half, xc] = msg[a, half, xc]

    def contract(a, half):
        pltpu.make_async_copy(
            msg.at[a, half, seven], rcv.at[a, half, seven], a_recv.at[2 * a + half]
        ).wait()
        r, c = iota((128, 128), 0), iota((128, 128), 1)
        pick = one_hot(c == (r & 7) * 16 + 2 * (r >> 4) + ((r >> 3) & 1))
        high, low = split(rcv[a, half].reshape(128, 768))
        high = mm(pick, high).astype(BF16)
        low = mm(pick, low).astype(BF16)
        both = jnp.concatenate([high, low], axis=0)

        @pl.loop(0, COL)
        def _(q):
            to_row = lax.rem(y + q, COL)
            at = pl.ds(pl.multiple_of(to_row * 256, 256), 256)
            into = pl.ds(to_row * ROW, ROW)
            part = mm_nt(whi[half, at, :], both)
            part = part[:, :128] + (part[:, 128:] + mm_nt(wlo[half, at, :], high))
            part = part.reshape(ROW, 32, 128)
            if half == 0:
                ct[a, into] = part
            else:
                ct[a, into] += part

                @pl.loop(0, ROW)
                def _(n):
                    to = to_row * ROW + lax.rem(xc + n, ROW)

                    @pl.when(to != d)
                    def _():
                        pltpu.make_async_remote_copy(
                            src_ref=ct.at[a, to], dst_ref=rs.at[a, d], send_sem=r_send.at[a], recv_sem=r_recv.at[a],
                            device_id={"amp": to, "int": z}, device_id_type=MESH,
                        ).start()

        if half == 1:
            rs[a, d] = ct[a, d]

    others = pl.ds(0, PLANE - 1)

    def narrow(a):
        pltpu.make_async_copy(ct.at[a, others], rs.at[a, others], r_recv.at[a]).wait()
        rows = []
        for row in range(COL):
            total = rs[a, row * ROW]
            for n in range(1, ROW):
                total += rs[a, row * ROW + n]
            rows.append(total)
        zs[:, 16 * a : 16 * a + 16, :] = jnp.concatenate(rows, axis=0).T.reshape(INT, 16, 128)

    def w_rest(way, halves):
        for h in halves:
            w_arrived(way, h, 1)

    w_rest(RIGHT, (1,))
    w_step(lax.rem(y + 3, COL))
    last(0)
    process(0, 4)
    event(1, 1, 0)
    regroup(0, 0)
    event(1, 1, 1)
    regroup(0, 1)
    event(1, 2, 0)
    w_rest(LEFT, (0,))
    w_step(lax.rem(y + 1, COL))
    event(1, 2, 1)
    process(1, 0)
    process(1, -1)
    process(1, 1)
    event(1, 3, 0)
    begin(2)
    w_arrived(RIGHT, 0, 2)
    w_arrived(LEFT, 1, 2)
    w_step(lax.rem(y + 2, COL))
    event(1, 3, 1)
    process(1, -2)
    process(1, 2)
    process(1, -3)
    process(1, 3)
    last(1)
    process(1, 4)
    event(2, 1, 0)
    regroup(1, 0)
    event(2, 1, 1)
    contract(0, 0)
    event(2, 2, 0)
    contract(0, 1)
    event(2, 2, 1)
    process(2, 0)
    process(2, -1)
    event(2, 3, 0)
    contract(1, 0)
    event(2, 3, 1)
    process(2, 1)
    process(2, -2)
    process(2, 2)
    process(2, -3)
    process(2, 3)
    last(2)
    process(2, 4)
    regroup(1, 1)
    lad_ref[:, 0:800] = acc0[:192, :]
    store_0 = pltpu.make_async_copy(lad_ref.at[:, pl.ds(0, 768)], lad_hbm.at[:, pl.ds(0, 768)], out_sem.at[0])
    store_0.start()
    lad_ref[:, 800:1200] = acc1[:192, :]
    lad_ref[:, 1200:1600] = acc2[:192, :]
    store_1 = pltpu.make_async_copy(lad_ref.at[:, pl.ds(768, 832)], lad_hbm.at[:, pl.ds(768, 832)], out_sem.at[1])
    store_1.start()
    narrow(0)

    sub, lane = iota((32, 128), 0), iota((32, 128), 1)
    row_label = jnp.where(lane < 64, occ_ref[2 * z], occ_ref[2 * z + 1])
    col_label = jnp.zeros((32, 128), jnp.int32) + occ_ref[d // 2]
    first = 32 * lax.rem(d, 2)

    def label_step(b, both):
        rows, cols = both
        rows = jnp.where((lane & 63) == b, rows ^ vir_ref[b], rows)
        cols = jnp.where(sub + first == b, cols ^ vir_ref[b], cols)
        return rows, cols

    row_label, col_label = lax.fori_loop(0, 64, label_step, (row_label, col_label))
    mask[...] = jnp.where(row_label == col_label, 1.0, 0.0).astype(F32)

    contract(1, 1)
    narrow(1)

    @pl.loop(1, INT)
    def _(j):
        up = lax.rem(z + j, INT)
        pltpu.make_async_remote_copy(
            src_ref=zs.at[up], dst_ref=zr.at[z], send_sem=z_sem.at[0], recv_sem=z_sem.at[1],
            device_id=in_stack(j), device_id_type=MESH,
        ).start()

    zr[z] = zs[z]
    pltpu.make_async_copy(zs.at[seven], zr.at[seven], z_sem.at[1]).wait()
    total = zr[0]
    for n in range(1, INT):
        total += zr[n]
    total = total.T
    m, r = iota((32, 128), 0), iota((32, 128), 1)
    kept = jnp.zeros((32, 128), F32)
    for row in range(COL):
        match = ((m >> 3) & 1 == r >> 6) & (m >> 4 == r & 1) & (m & 7 == (r >> 1) & 7) & ((r >> 4) & 3 == row)
        kept += jnp.dot(
            total[32 * row : 32 * row + 32], jnp.where(match, 1.0, 0.0).astype(F32),
            precision=lax.Precision.HIGHEST, preferred_element_type=F32,
        )
    sum_ref[...] = jnp.where(mask[...] > 0.5, kept, jnp.zeros_like(kept))

    for copy in started:
        copy.wait_send()
    pltpu.make_async_copy(s_buf.at[seven], t_buf.at[seven], s_sem.at[0]).wait()
    pltpu.make_async_copy(v_buf.at[seven], v_buf.at[seven], u_sem.at[0]).wait()
    for a in range(2):
        for half in range(2):
            pltpu.make_async_copy(
                msg.at[a, half, seven], rcv.at[a, half, seven], a_send.at[2 * a + half]
            ).wait()
        pltpu.make_async_copy(ct.at[a, others], rs.at[a, others], r_send.at[a]).wait()
    pltpu.make_async_copy(zs.at[seven], zr.at[seven], z_sem.at[0]).wait()
    store_0.wait()
    store_1.wait()


def hand_on(lad_in, sum_in, lad_out, sum_out, held, held_sum, sem):
    moves = [(sum_in, held_sum, sum_out, 8)]
    for n in range(8):
        rows = pl.ds(24 * n, 24)
        moves.append((lad_in.at[rows, :], held.at[rows, :], lad_out.at[rows, :], n))
    loads = [pltpu.make_async_copy(a, b, sem.at[n]) for a, b, _, n in moves]
    stores = [pltpu.make_async_copy(b, c, sem.at[9 + n]) for _, b, c, n in moves]
    for copy in loads:
        copy.start()
    for load, store in zip(loads, stores):
        load.wait()
        store.start()
    for copy in stores:
        copy.wait()


def per_device(amplitudes, slab_integrals, cycle_integrals, occ_irrep, vir_irrep):
    vmem = pl.BlockSpec(memory_space=pltpu.VMEM)
    smem = pl.BlockSpec(memory_space=pltpu.SMEM)
    anywhere = pl.BlockSpec(memory_space=pl.ANY)
    dma = pltpu.SemaphoreType.DMA
    ladder, sums = pl.pallas_call(
        body,
        out_shape=(
            jax.ShapeDtypeStruct((192, 1600), F32),
            jax.ShapeDtypeStruct((32, 128), F32),
        ),
        in_specs=[anywhere] * 3 + [smem] * 2,
        out_specs=(anywhere, vmem),
        scratch_shapes=[
            pltpu.VMEM((192, 1024), F32),
            pltpu.VMEM((12, 25, 1024), F32),
            pltpu.VMEM((192, 1600), F32),
            pltpu.VMEM((INT, 1600, 128), F32),
            pltpu.VMEM((INT, 384, 384), BF16),
            pltpu.VMEM((384, 800), F32),
            pltpu.VMEM((384, 400), F32),
            pltpu.VMEM((384, 400), F32),
            pltpu.VMEM((400, 512), BF16),
            pltpu.VMEM((INT, 32, 128), F32),
            pltpu.VMEM((INT, 32, 128), F32),
            pltpu.VMEM((192, 128), F32),
            pltpu.VMEM((INT, 192, 128), F32),
            pltpu.VMEM((COL, 304, 1024), F32),
            pltpu.VMEM((384, 1024), F32),
            pltpu.VMEM((2, 1024, 768), BF16),
            pltpu.VMEM((2, 1024, 768), BF16),
            pltpu.VMEM((2, 2, ROW, 16, 768), F32),
            pltpu.VMEM((2, 2, ROW, 16, 768), F32),
            pltpu.VMEM((2, PLANE, 32, 128), F32),
            pltpu.VMEM((2, PLANE, 32, 128), F32),
            pltpu.VMEM((INT, 32, 128), F32),
            pltpu.VMEM((INT, 32, 128), F32),
            pltpu.VMEM((32, 128), F32),
            dma((3,)),
            dma((2,)),
            dma((96,)),
            dma((96,)),
            dma((2,)),
            dma((2,)),
            dma((6,)),
            dma((6,)),
            dma((4,)),
            dma((4,)),
            dma((2,)),
            dma((2,)),
            dma((2,)),
        ],
        compiler_params=pltpu.CompilerParams(
            collective_id=0, has_side_effects=True, vmem_limit_bytes=58 * 1024 * 1024
        ),
        cost_estimate=pl.CostEstimate(flops=8_000_000_000, bytes_accessed=8_000_000, transcendentals=0),
    )(amplitudes, slab_integrals.T, cycle_integrals, occ_irrep, vir_irrep)
    ladder, sums = pl.pallas_call(
        hand_on,
        out_shape=(
            jax.ShapeDtypeStruct((192, 1600), F32),
            jax.ShapeDtypeStruct((32, 128), F32),
        ),
        in_specs=[anywhere] * 2,
        out_specs=(anywhere, anywhere),
        scratch_shapes=[pltpu.VMEM((192, 1600), F32), pltpu.VMEM((32, 128), F32), dma((18,))],
    )(ladder, sums)
    return ladder, sums.T


def solution(mesh):
    in_specs = (P("int", None), P("int", "amp"), P("int", "amp", None), P(), P())
    out_specs = (P("int", "amp"), P("int", "amp"))
    return jax.shard_map(
        per_device, mesh=mesh, in_specs=in_specs, out_specs=out_specs, check_vma=False
    )
```

```python
import jax
import jax.numpy as jnp
from jax import lax
from jax.experimental import pallas as pl
from jax.experimental.pallas import tpu as pltpu
from jax.sharding import PartitionSpec as P

F32 = jnp.float32
BF16 = jnp.bfloat16
MESH = pl.DeviceIdType.MESH

INT = 8
ROW = 8
COL = 4
CHIPS = 16
WIDTHS = (800, 400, 400)
STARTS = (0, 800, 1200)
PIECES = tuple(
    tuple((start + width * q // 4 // 8 * 8, (width * (q + 1) // 4 // 8 - width * q // 4 // 8) * 8) for q in range(4))
    for start, width in zip(STARTS, WIDTHS)
)
RIGHT, LEFT = 0, 1


def iota(shape, dim):
    return lax.broadcasted_iota(jnp.int32, shape, dim)


def split(x):
    high = x.astype(BF16)
    return high, (x - high.astype(F32)).astype(BF16)


def mm(a, b):
    return jnp.dot(a, b, preferred_element_type=F32)


def mm_nt(a, b):
    return lax.dot_general(a, b, (((1,), (1,)), ((), ())), preferred_element_type=F32)


def one_hot(match):
    return jnp.where(match, 1.0, 0.0).astype(BF16)


def body(
    amp_hbm, slab_hbm, w_hbm, occ_ref, vir_ref,
    lad_hbm, sum_ref,
    amp_ref, w_ref, lad_ref, slab, a3, acc0, acc1, acc2, table, s_buf, t_buf, u_buf, v_buf,
    wg, wpad, whi, wlo, msg, rcv, ct, cs, rs, zs, zr, mask,
    in_sem, out_sem, ag_send, ag_recv, s_sem, u_sem, w_send, w_recv, a_send, a_recv, c_send, c_recv, r_send, r_recv, z_sem,
):
    d = lax.axis_index("amp")
    z = lax.axis_index("int")
    y = d // ROW
    xc = lax.rem(d, ROW)
    core = lax.rem(d, 2)
    chip = d // 2
    accs = (acc0, acc1, acc2)

    def around(step):
        return lax.rem(z + step + INT, INT)

    def in_row(j):
        return {"amp": y * ROW + lax.rem(xc + j, ROW), "int": z}

    def in_col(j):
        return {"amp": lax.rem(y + j, COL) * ROW + xc, "int": z}

    def in_stack(j):
        return {"amp": d, "int": lax.rem(z + j, INT)}

    barrier = pltpu.get_barrier_semaphore()

    for j in (1, INT - 1, 2, INT - 2, 3, INT - 3, 4):
        pl.semaphore_signal(barrier, inc=1, device_id=in_stack(j), device_id_type=MESH)
    for j in (1, COL - 1):
        pl.semaphore_signal(barrier, inc=1, device_id=in_col(j), device_id_type=MESH)

    @pl.loop(1, ROW)
    def _(j):
        pl.semaphore_signal(barrier, inc=1, device_id=in_row(j), device_id_type=MESH)

    load_amp = pltpu.make_async_copy(amp_hbm, amp_ref, in_sem.at[0])
    load_slab = pltpu.make_async_copy(slab_hbm, slab.at[z], in_sem.at[1])
    load_w = pltpu.make_async_copy(w_hbm, w_ref, in_sem.at[2])
    load_amp.start()
    load_slab.start()
    load_w.start()

    def place(c, q):
        return pl.ds(*PIECES[c][q])

    def piece(way, c, j, q):
        hop = 1 if way == RIGHT else -1
        part = slab.at[around(-hop * (j - 1)), place(c, q), :]
        source = slab_hbm.at[place(c, q), :] if j == 1 else part
        k = ((way * 3 + c) * 4 + (j - 1)) * 4 + q
        return pltpu.make_async_remote_copy(
            src_ref=source, dst_ref=part, send_sem=ag_send.at[k], recv_sem=ag_recv.at[k],
            device_id={"amp": d, "int": around(hop)}, device_id_type=MESH,
        )

    started = []

    def launch(way, c, j, q):
        copy = piece(way, c, j, q)
        copy.start()
        started.append(copy)

    def arrived(way, c, j, q):
        hop = 1 if way == RIGHT else -1
        part = slab.at[around(-hop * j), place(c, q), :]
        k = ((way * 3 + c) * 4 + (j - 1)) * 4 + q
        pltpu.make_async_copy(part, part, ag_recv.at[k]).wait()

    order = ((RIGHT, 0), (LEFT, 3), (RIGHT, 1), (LEFT, 2)), ((RIGHT, 2), (LEFT, 1), (RIGHT, 3), (LEFT, 0))

    def begin(c):
        for way, q in order[0] + order[1]:
            launch(way, c, 1, q)

    def event(c, j, g):
        for way, q in order[g]:
            arrived(way, c, j, q)
            if j < 3 or g == 0:
                launch(way, c, j + 1, q)

    def last(c):
        for way, q in order[0]:
            arrived(way, c, 4, q)

    def process(c, step):
        origin = around(step)
        a_block = a3[origin]
        tiles = ((0, 512), (512, 288)) if c == 0 else ((0, 400),)
        for col, n in tiles:
            high, low = split(slab[origin, STARTS[c] + col : STARTS[c] + col + n, :])
            part = mm_nt(a_block, jnp.concatenate([high, high, low], axis=1))
            if step == 0:
                accs[c][:, col : col + n] = part
            else:
                accs[c][:, col : col + n] += part

    load_amp.wait()
    here = pl.ds(pl.multiple_of(xc * 128, 128), 128)
    r, c = iota((256, 192), 0), iota((256, 192), 1)
    pick = one_hot((c == 96 * ((r >> 4) & 1) + 12 * (r >> 5) + (r & 15)) & ((r & 15) < 12))
    high, low = split(amp_ref[:, here])
    s_buf[...] = (mm(pick, high) + mm(pick, low)).reshape(INT, 32, 128)
    pl.semaphore_wait(barrier, INT - 1 + 2 + ROW - 1)

    @pl.loop(1, INT)
    def _(j):
        up = lax.rem(z + j, INT)
        pltpu.make_async_remote_copy(
            src_ref=s_buf.at[up], dst_ref=t_buf.at[z], send_sem=s_sem.at[0], recv_sem=s_sem.at[1],
            device_id=in_stack(j), device_id_type=MESH,
        ).start()

    begin(0)
    t_buf[z] = s_buf[z]

    load_w.wait()
    for k in range(12):
        wg[y, 25 * k : 25 * k + 25, :] = w_ref[k]
    wg[y, 300:304, :] = jnp.zeros((4, 1024), F32)

    def w_piece(way, h, hop_from):
        hop = 1 if way == RIGHT else 3
        part = wg.at[lax.rem(y + (4 - hop) * hop_from, COL), pl.ds(152 * h, 152), :]
        k = way * 3 + (2 if hop_from else h)
        return pltpu.make_async_remote_copy(
            src_ref=part, dst_ref=part, send_sem=w_send.at[k], recv_sem=w_recv.at[k],
            device_id=in_col(hop), device_id_type=MESH,
        )

    def w_arrived(way, h, hops):
        hop = 1 if way == RIGHT else 3
        part = wg.at[lax.rem(y + (4 - hop) * hops, COL), pl.ds(152 * h, 152), :]
        pltpu.make_async_copy(part, part, w_recv.at[way * 3 + (2 if hops == 2 else h)]).wait()

    def w_launch(*which):
        copy = w_piece(*which)
        copy.start()
        started.append(copy)

    w_launch(RIGHT, 0, 0)
    w_launch(LEFT, 1, 0)
    w_launch(RIGHT, 1, 0)
    w_launch(LEFT, 0, 0)

    seven = pl.ds(0, 7)

    r, c = iota((400, 512), 0), iota((400, 512), 1)
    table[...] = one_hot((r == 200 * (c >> 8) + 25 * ((c >> 5) & 7) + (c & 31)) & ((c & 31) < 25))

    def w_step(block):
        for k in range(12):
            wpad[32 * k : 32 * k + 25, :] = wg[block, 25 * k : 25 * k + 25, :]
        into = block // 2
        lanes = lax.rem(block, 2) * 384

        @pl.loop(0, 8)
        def _(i):
            at = pl.ds(pl.multiple_of(i * 128, 128), 128)
            for k4 in range(3):
                high, low = split(wpad[128 * k4 : 128 * k4 + 128, at].T)
                to = pl.ds(pl.multiple_of(lanes + 128 * k4, 128), 128)
                whi[into, at, to] = high
                wlo[into, at, to] = low

    event(0, 1, 0)
    pltpu.make_async_copy(s_buf.at[seven], t_buf.at[seven], s_sem.at[1]).wait()
    r, c = iota((192, 256), 0), iota((192, 256), 1)
    pick = one_hot(c == 32 * ((r >> 1) & 7) + 16 * (r & 1) + (r >> 4))
    high, low = split(t_buf[...].reshape(256, 128))
    u_buf[...] = mm(pick, high) + mm(pick, low)

    @pl.loop(1, ROW)
    def _(j):
        pltpu.make_async_remote_copy(
            src_ref=u_buf, dst_ref=v_buf.at[xc], send_sem=u_sem.at[0], recv_sem=u_sem.at[1],
            device_id=in_row(j), device_id_type=MESH,
        ).start()

    v_buf[xc] = u_buf[...]
    event(0, 1, 1)
    for o in range(INT):
        high, low = split(amp_ref[:, 128 * o : 128 * o + 128])
        a3[o, :192, 0:128] = high
        a3[o, :192, 128:256] = low
        a3[o, :192, 256:384] = high

    wpad[...] = jnp.zeros_like(wpad)
    event(0, 2, 0)
    w_step(y)
    event(0, 2, 1)
    w_arrived(RIGHT, 0, 1)
    w_launch(RIGHT, 0, 1)
    w_arrived(LEFT, 1, 1)
    w_launch(LEFT, 1, 1)
    pltpu.make_async_copy(v_buf.at[seven], v_buf.at[seven], u_sem.at[1]).wait()

    @pl.loop(0, INT)
    def _(o):
        high, low = split(v_buf[o])
        a3[o, 192:, 0:128] = high
        a3[o, 192:, 128:256] = low
        a3[o, 192:, 256:384] = high
    load_slab.wait()
    process(0, 0)
    process(0, -1)
    process(0, 1)
    event(0, 3, 0)
    begin(1)
    process(0, -2)
    process(0, 2)
    event(0, 3, 1)
    process(0, -3)
    process(0, 3)

    def regroup(a, half):
        source = acc0[192:, 400 * half : 400 * half + 400] if a == 0 else accs[1 + half][192:, :]
        high, low = split(source)
        spaced = mm(high, table[...]) + mm(low, table[...])
        lane = iota((16, 128), 1)
        even = (lane & 32) == 0
        lower = (lane & 64) == 0
        for t in range(4):
            for k4 in range(3):
                x = [spaced[(4 * k4 + q) * 16 : (4 * k4 + q) * 16 + 16, 128 * t : 128 * t + 128] for q in range(4)]
                v = [None] * 4
                for q in (0, 2):
                    v[q] = jnp.where(even, x[q], pltpu.roll(x[q + 1], 32, 1))
                    v[q + 1] = jnp.where(even, pltpu.roll(x[q], 96, 1), x[q + 1])
                o = [None] * 4
                for q in (0, 1):
                    o[q] = jnp.where(lower, v[q], pltpu.roll(v[q + 2], 64, 1))
                    o[q + 2] = jnp.where(lower, pltpu.roll(v[q], 64, 1), v[q + 2])
                at = 384 * (t // 2) + 128 * k4
                for s in range(4):
                    msg[a, half, 4 * (t % 2) + s, :, at : at + 128] = o[s]

        @pl.loop(1, ROW)
        def _(j):
            to = lax.rem(xc + j, ROW)
            pltpu.make_async_remote_copy(
                src_ref=msg.at[a, half, to], dst_ref=rcv.at[a, half, xc],
                send_sem=a_send.at[2 * a + half], recv_sem=a_recv.at[2 * a + half],
                device_id=in_row(j), device_id_type=MESH,
            ).start()

        rcv[a, half, xc] = msg[a, half, xc]

    def contract(a, half):
        pltpu.make_async_copy(
            msg.at[a, half, seven], rcv.at[a, half, seven], a_recv.at[2 * a + half]
        ).wait()
        r, c = iota((128, 128), 0), iota((128, 128), 1)
        pick = one_hot(c == (r & 7) * 16 + 2 * (r >> 4) + ((r >> 3) & 1))
        high, low = split(rcv[a, half].reshape(128, 768))
        high = mm(pick, high).astype(BF16)
        low = mm(pick, low).astype(BF16)
        both = jnp.concatenate([high, low], axis=0)

        @pl.loop(0, COL)
        def _(q):
            to_row = lax.rem(y + q, COL)
            at = pl.ds(pl.multiple_of(to_row * 256, 256), 256)
            part = mm_nt(whi[half, at, :], both)
            part = part[:, :128] + (part[:, 128:] + mm_nt(wlo[half, at, :], high))
            part = part.reshape(COL, 2, 32, 128)
            into = pl.ds(to_row * COL, COL)
            for n in range(2):
                if half == 0:
                    ct[a, n, into] = part[:, n]
                else:
                    ct[a, n, into] += part[:, n]

        if half == 1:
            pltpu.make_async_remote_copy(
                src_ref=ct.at[a, 1 - core], dst_ref=cs.at[a], send_sem=c_send.at[a], recv_sem=c_recv.at[a],
                device_id={"amp": d + 1 - 2 * core, "int": z}, device_id_type=MESH,
            ).start()

    others = pl.ds(0, CHIPS - 1)

    def spread(a):
        pltpu.make_async_copy(cs.at[a], cs.at[a], c_recv.at[a]).wait()

        @pl.loop(1, CHIPS)
        def _(n):
            to = lax.rem(chip + n, CHIPS)
            ct[a, core, to] += cs[a, to]
            pltpu.make_async_remote_copy(
                src_ref=ct.at[a, core, to], dst_ref=rs.at[a, chip], send_sem=r_send.at[a], recv_sem=r_recv.at[a],
                device_id={"amp": to * 2 + core, "int": z}, device_id_type=MESH,
            ).start()

        rs[a, chip] = ct[a, core, chip] + cs[a, chip]

    def narrow(a):
        pltpu.make_async_copy(rs.at[a, others], rs.at[a, others], r_recv.at[a]).wait()
        rows = []
        for row in range(COL):
            total = rs[a, row * COL]
            for n in range(1, COL):
                total += rs[a, row * COL + n]
            rows.append(total)
        zs[:, 16 * a : 16 * a + 16, :] = jnp.concatenate(rows, axis=0).T.reshape(INT, 16, 128)

    def w_rest(way, halves):
        for h in halves:
            w_arrived(way, h, 1)

    w_rest(RIGHT, (1,))
    w_step(lax.rem(y + 3, COL))
    last(0)
    process(0, 4)
    event(1, 1, 0)
    regroup(0, 0)
    event(1, 1, 1)
    regroup(0, 1)
    event(1, 2, 0)
    w_rest(LEFT, (0,))
    w_step(lax.rem(y + 1, COL))
    event(1, 2, 1)
    process(1, 0)
    process(1, -1)
    process(1, 1)
    event(1, 3, 0)
    begin(2)
    w_arrived(RIGHT, 0, 2)
    w_arrived(LEFT, 1, 2)
    w_step(lax.rem(y + 2, COL))
    event(1, 3, 1)
    process(1, -2)
    process(1, 2)
    process(1, -3)
    process(1, 3)
    last(1)
    process(1, 4)
    event(2, 1, 0)
    regroup(1, 0)
    event(2, 1, 1)
    contract(0, 0)
    event(2, 2, 0)
    contract(0, 1)
    event(2, 2, 1)
    process(2, 0)
    process(2, -1)
    event(2, 3, 0)
    spread(0)
    contract(1, 0)
    event(2, 3, 1)
    process(2, 1)
    process(2, -2)
    process(2, 2)
    process(2, -3)
    process(2, 3)
    last(2)
    process(2, 4)
    regroup(1, 1)
    lad_ref[:, 0:800] = acc0[:192, :]
    store_0 = pltpu.make_async_copy(lad_ref.at[:, pl.ds(0, 768)], lad_hbm.at[:, pl.ds(0, 768)], out_sem.at[0])
    store_0.start()
    lad_ref[:, 800:1200] = acc1[:192, :]
    lad_ref[:, 1200:1600] = acc2[:192, :]
    store_1 = pltpu.make_async_copy(lad_ref.at[:, pl.ds(768, 832)], lad_hbm.at[:, pl.ds(768, 832)], out_sem.at[1])
    store_1.start()
    narrow(0)

    sub, lane = iota((32, 128), 0), iota((32, 128), 1)
    row_label = jnp.where(lane < 64, occ_ref[2 * z], occ_ref[2 * z + 1])
    col_label = jnp.zeros((32, 128), jnp.int32) + occ_ref[d // 2]
    first = 32 * lax.rem(d, 2)

    def label_step(b, both):
        rows, cols = both
        rows = jnp.where((lane & 63) == b, rows ^ vir_ref[b], rows)
        cols = jnp.where(sub + first == b, cols ^ vir_ref[b], cols)
        return rows, cols

    row_label, col_label = lax.fori_loop(0, 64, label_step, (row_label, col_label))
    mask[...] = jnp.where(row_label == col_label, 1.0, 0.0).astype(F32)

    contract(1, 1)
    spread(1)
    narrow(1)

    @pl.loop(1, INT)
    def _(j):
        up = lax.rem(z + j, INT)
        pltpu.make_async_remote_copy(
            src_ref=zs.at[up], dst_ref=zr.at[z], send_sem=z_sem.at[0], recv_sem=z_sem.at[1],
            device_id=in_stack(j), device_id_type=MESH,
        ).start()

    zr[z] = zs[z]
    pltpu.make_async_copy(zs.at[seven], zr.at[seven], z_sem.at[1]).wait()
    total = zr[0]
    for n in range(1, INT):
        total += zr[n]
    total = total.T
    m, r = iota((32, 128), 0), iota((32, 128), 1)
    kept = jnp.zeros((32, 128), F32)
    for row in range(COL):
        match = ((m >> 3) & 1 == r >> 6) & (m >> 4 == r & 1) & (m & 7 == (r >> 1) & 7) & ((r >> 4) & 3 == row)
        kept += jnp.dot(
            total[32 * row : 32 * row + 32], jnp.where(match, 1.0, 0.0).astype(F32),
            precision=lax.Precision.HIGHEST, preferred_element_type=F32,
        )
    sum_ref[...] = jnp.where(mask[...] > 0.5, kept, jnp.zeros_like(kept))

    for copy in started:
        copy.wait_send()
    pltpu.make_async_copy(s_buf.at[seven], t_buf.at[seven], s_sem.at[0]).wait()
    pltpu.make_async_copy(v_buf.at[seven], v_buf.at[seven], u_sem.at[0]).wait()
    for a in range(2):
        for half in range(2):
            pltpu.make_async_copy(
                msg.at[a, half, seven], rcv.at[a, half, seven], a_send.at[2 * a + half]
            ).wait()
        pltpu.make_async_copy(cs.at[a], cs.at[a], c_send.at[a]).wait()
        pltpu.make_async_copy(rs.at[a, others], rs.at[a, others], r_send.at[a]).wait()
    pltpu.make_async_copy(zs.at[seven], zr.at[seven], z_sem.at[0]).wait()
    store_0.wait()
    store_1.wait()


def hand_on(lad_in, sum_in, lad_out, sum_out, held, held_sum, sem):
    moves = [(sum_in, held_sum, sum_out, 8)]
    for n in range(8):
        rows = pl.ds(24 * n, 24)
        moves.append((lad_in.at[rows, :], held.at[rows, :], lad_out.at[rows, :], n))
    loads = [pltpu.make_async_copy(a, b, sem.at[n]) for a, b, _, n in moves]
    stores = [pltpu.make_async_copy(b, c, sem.at[9 + n]) for _, b, c, n in moves]
    for copy in loads:
        copy.start()
    for load, store in zip(loads, stores):
        load.wait()
        store.start()
    for copy in stores:
        copy.wait()


def per_device(amplitudes, slab_integrals, cycle_integrals, occ_irrep, vir_irrep):
    vmem = pl.BlockSpec(memory_space=pltpu.VMEM)
    smem = pl.BlockSpec(memory_space=pltpu.SMEM)
    anywhere = pl.BlockSpec(memory_space=pl.ANY)
    dma = pltpu.SemaphoreType.DMA
    ladder, sums = pl.pallas_call(
        body,
        out_shape=(
            jax.ShapeDtypeStruct((192, 1600), F32),
            jax.ShapeDtypeStruct((32, 128), F32),
        ),
        in_specs=[anywhere] * 3 + [smem] * 2,
        out_specs=(anywhere, vmem),
        scratch_shapes=[
            pltpu.VMEM((192, 1024), F32),
            pltpu.VMEM((12, 25, 1024), F32),
            pltpu.VMEM((192, 1600), F32),
            pltpu.VMEM((INT, 1600, 128), F32),
            pltpu.VMEM((INT, 384, 384), BF16),
            pltpu.VMEM((384, 800), F32),
            pltpu.VMEM((384, 400), F32),
            pltpu.VMEM((384, 400), F32),
            pltpu.VMEM((400, 512), BF16),
            pltpu.VMEM((INT, 32, 128), F32),
            pltpu.VMEM((INT, 32, 128), F32),
            pltpu.VMEM((192, 128), F32),
            pltpu.VMEM((INT, 192, 128), F32),
            pltpu.VMEM((COL, 304, 1024), F32),
            pltpu.VMEM((384, 1024), F32),
            pltpu.VMEM((2, 1024, 768), BF16),
            pltpu.VMEM((2, 1024, 768), BF16),
            pltpu.VMEM((2, 2, ROW, 16, 768), F32),
            pltpu.VMEM((2, 2, ROW, 16, 768), F32),
            pltpu.VMEM((2, 2, CHIPS, 32, 128), F32),
            pltpu.VMEM((2, CHIPS, 32, 128), F32),
            pltpu.VMEM((2, CHIPS, 32, 128), F32),
            pltpu.VMEM((INT, 32, 128), F32),
            pltpu.VMEM((INT, 32, 128), F32),
            pltpu.VMEM((32, 128), F32),
            dma((3,)),
            dma((2,)),
            dma((96,)),
            dma((96,)),
            dma((2,)),
            dma((2,)),
            dma((6,)),
            dma((6,)),
            dma((4,)),
            dma((4,)),
            dma((2,)),
            dma((2,)),
            dma((2,)),
            dma((2,)),
            dma((2,)),
        ],
        compiler_params=pltpu.CompilerParams(
            collective_id=0, has_side_effects=True, vmem_limit_bytes=58 * 1024 * 1024
        ),
        cost_estimate=pl.CostEstimate(flops=8_000_000_000, bytes_accessed=8_000_000, transcendentals=0),
    )(amplitudes, slab_integrals.T, cycle_integrals, occ_irrep, vir_irrep)
    ladder, sums = pl.pallas_call(
        hand_on,
        out_shape=(
            jax.ShapeDtypeStruct((192, 1600), F32),
            jax.ShapeDtypeStruct((32, 128), F32),
        ),
        in_specs=[anywhere] * 2,
        out_specs=(anywhere, anywhere),
        scratch_shapes=[pltpu.VMEM((192, 1600), F32), pltpu.VMEM((32, 128), F32), dma((18,))],
    )(ladder, sums)
    return ladder, sums.T


def solution(mesh):
    in_specs = (P("int", None), P("int", "amp"), P("int", "amp", None), P(), P())
    out_specs = (P("int", "amp"), P("int", "amp"))
    return jax.shard_map(
        per_device, mesh=mesh, in_specs=in_specs, out_specs=out_specs, check_vma=False
    )
```
